512 devices in a mesh: blk: 256 (over x_lo, z, y, core), rep: 2 (over x_hi).
Axes of the slice: x: 4 (x_hi: 2, x_lo: 2; x = x_hi * 2 + x_lo), y: 4, z: 16, core: 2. Of those that a mesh axis runs over, the one named last changes fastest.
Arguments:
- body_ids: int32 [131072], P('blk'), may hold values from 0 to 511, as said below
- body_centers: float32 [3, 512], replicated, may hold values from -20 to 20
- blob_offsets: float32 [3, 131072], P(None, 'blk'), may hold values from -24 to 24
- plan: int32 [4], replicated, may hold values from 1 to 255, as said below
- probes: float32 [3, 16, 131072], P(None, None, 'blk'), may hold values from -360 to 360
- previous_probes: float32 [3, 16, 131072], P(None, None, 'blk'), may hold values from -72 to 72
- previous_beta: float32 [16, 16], replicated, may hold values from -0.9 to 1.5, as said below
Outputs:
- next_probes: float32 [3, 16, 131072], P(None, None, 'blk')
The draws below stay inside these ranges and needn't reach their ends.
Inputs may be any that keep to these rules, and one draw needn't show every extreme that they name: The entries are distinct; in round r block k meets block k XOR plan[r]. `body_ids`: each of the 512 bodies has exactly 256 blobs. `previous_beta`: lower triangular, with diagonal entries from 0.5 to 1.5.
All inputs are finite; a program needn't handle non-finite values.
Results may differ from the reference program's by a relative error of at most 0.0049.
Values sent between devices are 32-bit elements; how exact they have to be, the bound alone decides.
No kernel may reach another device: no remote copies, remote signals or barrier semaphores. Data moves between devices by JAX's collectives and lax.ppermute only.
A program may use at most 64 MiB of HBM per device.

```python
import math
import jax
import jax.numpy as jnp
from jax import lax

BLK_DEV = 512
PROBES = 16
ROUNDS = 4
BODY_BLOBS = 256
BLOBS = 131072
BODIES = 512
N_BLK = 256


def draw_plan(key, part):
    key = jax.random.fold_in(key, 11)
    keys = jax.random.split(key, 2)
    block_total = BLOBS // BLK_DEV
    middle = jax.random.permutation(keys[0], block_total - 3)[:ROUNDS - 2] + 2
    ends = jnp.array([1, block_total - 1], dtype=jnp.int32)
    values = jnp.concatenate([ends, middle.astype(jnp.int32)])
    return jax.random.permutation(keys[1], values).astype(jnp.int32)


def draw_body_ids(key, part):
    key = jax.random.fold_in(key, 17)
    order = jax.random.permutation(key, BLOBS)
    return (order // BODY_BLOBS).astype(jnp.int32)


def draw_probes(key, part):
    key = jax.random.fold_in(key, 23)
    keys = jax.random.split(key, 4)
    base = jnp.clip(jax.random.normal(keys[0], (3, PROBES, BLOBS), jnp.float32), -4.0, 4.0)
    column = jnp.exp(jax.random.uniform(keys[2], (PROBES,), jnp.float32, 0.0, math.log(10.0)))
    rising = 1.0 + 2.0 * jnp.arange(BLOBS, dtype=jnp.float32) / BLOBS
    row_scale = rising * jnp.exp(jax.random.uniform(keys[3], (BLOBS,), jnp.float32, 0.0, math.log(3.0)))
    return base * column[None, :, None] * row_scale[None, None, :]


def draw_previous_beta(key, part):
    key = jax.random.fold_in(key, 37)
    keys = jax.random.split(key, 2)
    diagonal = jax.random.uniform(keys[0], (PROBES,), jnp.float32, 0.5, 1.5)
    lower_part = 0.3 * jnp.clip(jax.random.normal(keys[1], (PROBES, PROBES), jnp.float32), -3.0, 3.0)
    indices = jnp.arange(PROBES)
    below = indices[:, None] > indices[None, :]
    return jnp.where(below, lower_part, 0.0) + jnp.diag(diagonal)


def block_levels(key, shape, shards, low, high):
    def one(position, shards_of):
        draws = jax.random.uniform(jax.random.fold_in(jax.random.fold_in(key, 6), position), (shards_of,), jnp.float32, low / len(shards), high / len(shards))
        return jnp.repeat(jnp.exp(draws), shape[position] // shards_of).reshape((-1,) + (1,) * (len(shape) - position - 1))

    loudness = one(*shards[0])
    for cut in shards[1:]:
        loudness = loudness * one(*cut)
    return loudness


def centred(stream_key, extent, width, most, cuts=(), kind=jnp.bfloat16):
    drawn = width * jax.random.normal(stream_key, extent, jnp.float32)
    if cuts:
        drawn = drawn * block_levels(stream_key, extent, cuts, -0.22, 0.18)
    return jnp.clip(drawn, -most, most).astype(kind)


def setup_inputs(seed: int = 0) -> dict:
    key_of = jax.random.split(jax.random.key(seed), 8)
    return {
        "body_ids": draw_body_ids(jax.random.fold_in(key_of[7], 71), 0),
        "body_centers": jnp.clip(jax.random.uniform(key_of[1], (3, BODIES), jnp.float32, -20.0, 20.0), -20.0, 20.0),
        "blob_offsets": centred(key_of[2], (3, BLOBS), 4.0, 24.0, ((1, 256),), jnp.float32),
        "plan": draw_plan(jax.random.fold_in(key_of[7], 71), 0),
        "probes": draw_probes(jax.random.fold_in(key_of[7], 71), 0),
        "previous_probes": centred(key_of[5], (3, PROBES, BLOBS), 12.0, 72.0, ((2, 256),), jnp.float32),
        "previous_beta": draw_previous_beta(jax.random.fold_in(key_of[7], 71), 0),
    }


blob_radius = 1.0
precise = lax.Precision.HIGHEST

def mobility_kernel(targets, sources):
    separation = targets[:, :, None] - sources[:, None, :]
    square = lax.optimization_barrier(jnp.sum(separation * separation, axis=0))
    safe_square = jnp.where(square > 0.0, square, 1.0)
    inverse = 1.0 / jnp.sqrt(safe_square)
    distance = jnp.sqrt(square)
    radius_ratio = blob_radius * inverse
    far_isotropic = 0.75 * radius_ratio * (1.0 + 2.0 / 3.0 * radius_ratio * radius_ratio)
    far_dyadic = 0.75 * radius_ratio * (1.0 - 2.0 * radius_ratio * radius_ratio) * inverse * inverse
    near_isotropic = 1.0 - 9.0 / 32.0 * distance / blob_radius
    near_dyadic = 3.0 / 32.0 / blob_radius * inverse
    far_mask = distance > 2.0 * blob_radius
    isotropic = jnp.where(far_mask, far_isotropic, near_isotropic)
    dyadic = jnp.where(far_mask, far_dyadic, near_dyadic)
    outer_part = dyadic[None, None] * separation[:, None] * separation[None, :]
    identity = jnp.eye(3, dtype=jnp.float32)
    return outer_part + identity[:, :, None, None] * isotropic[None, None]

def tile_product(targets, sources, source_vectors, target_vectors, want_back):
    row_count = targets.shape[1]
    row_width = min(32, row_count)
    pieces = row_count // row_width
    target_pieces = jnp.moveaxis(targets.reshape(3, pieces, row_width), 1, 0)
    vector_pieces = jnp.moveaxis(target_vectors.reshape(3, target_vectors.shape[1], pieces, row_width), 2, 0)
    initial = jnp.zeros(source_vectors.shape, jnp.float32)

    def scan_step(running, scan_item):
        target_piece, vector_piece = scan_item
        kernel = mobility_kernel(target_piece, sources)
        forward = jnp.einsum('abij,bpj->api', kernel, source_vectors, precision=precise)
        if want_back:
            running = running + jnp.einsum('abij,bpi->apj', kernel, vector_piece, precision=precise)
        return (running, forward)
    backward, forward = lax.scan(scan_step, initial, (target_pieces, vector_pieces))
    forward = jnp.moveaxis(forward, 0, 2).reshape(3, source_vectors.shape[1], row_count)
    return (forward, backward)

def reference(body_ids, body_centers, blob_offsets, plan, probes, previous_probes, previous_beta):
    positions = jnp.take(body_centers, body_ids, axis=1) + blob_offsets
    blob_total = positions.shape[1]
    block_size = blob_total // N_BLK

    def block_velocity(block_index):
        start = (block_index * block_size).astype(jnp.int32)
        home_positions = lax.dynamic_slice_in_dim(positions, start, block_size, 1)
        home_vectors = lax.dynamic_slice_in_dim(probes, start, block_size, 2)
        velocity = tile_product(home_positions, home_positions, home_vectors, home_vectors, False)[0]
        for rotation in range(ROUNDS):
            partner = jnp.bitwise_xor(block_index, plan[rotation])
            partner_start = (partner * block_size).astype(jnp.int32)
            partner_positions = lax.dynamic_slice_in_dim(positions, partner_start, block_size, 1)
            partner_vectors = lax.dynamic_slice_in_dim(probes, partner_start, block_size, 2)
            velocity = velocity + tile_product(home_positions, partner_positions, partner_vectors, home_vectors, False)[0]
        return velocity
    velocities = lax.map(block_velocity, jnp.arange(N_BLK, dtype=jnp.int32))
    velocity = jnp.moveaxis(velocities, 0, 2).reshape(3, PROBES, blob_total)
    normalizer = 1.0 / (3.0 * blob_total)
    projection = jnp.einsum('apj,aqj->pq', probes, velocity, precision=precise) * normalizer
    residual = velocity - jnp.einsum('pq,apj->aqj', projection, probes, precision=precise)
    residual = residual - jnp.einsum('qp,apj->aqj', previous_beta, previous_probes, precision=precise)
    gram_matrix = jnp.einsum('apj,aqj->pq', residual, residual, precision=precise) * normalizer
    factor = jnp.linalg.cholesky(gram_matrix)
    identity = jnp.eye(PROBES, dtype=jnp.float32)
    inverse_factor = jax.scipy.linalg.solve_triangular(factor, identity, lower=True)
    return jnp.einsum('qp,apj->aqj', inverse_factor, residual, precision=precise)
```

```python
import functools

import jax
import jax.numpy as jnp
from jax import lax
from jax.experimental import pallas as pl
from jax.experimental.pallas import tpu as pltpu
from jax.sharding import PartitionSpec as P

precise = lax.Precision.HIGHEST
pairs = ((0, 0), (1, 1), (2, 2), (0, 1), (0, 2), (1, 2))
vmem_bytes = 40 * 1024 * 1024


def three_parts(value):
    high = value.astype(jnp.bfloat16)
    rest = value - high.astype(jnp.float32)
    middle = rest.astype(jnp.bfloat16)
    low = (rest - middle.astype(jnp.float32)).astype(jnp.bfloat16)
    return high, middle, low


def dot_nt(left, right):
    return lax.dot_general(
        left, right, (((1,), (1,)), ((), ())), precision=precise,
        preferred_element_type=jnp.float32,
    )


def dot_nn(left, right):
    return lax.dot_general(
        left, right, (((1,), (0,)), ((), ())), precision=precise,
        preferred_element_type=jnp.float32,
    )


def reciprocal_root(square):
    guess = lax.rsqrt(square)
    return guess * (1.5 - 0.5 * square * guess * guess)


def fill_tile(kernel_ref, target_rows, source_columns, depth, slab):
    for start in range(0, depth, slab):
        rows = slice(start, start + slab)
        separation = [target_rows[a] - source_columns[a][rows] for a in range(3)]
        square = separation[0] * separation[0]
        square = square + separation[1] * separation[1]
        square = square + separation[2] * separation[2]
        inverse = reciprocal_root(jnp.where(square > 0.0, square, 1.0))
        inverse_square = inverse * inverse
        far = square > 4.0
        far_isotropic = inverse * (0.75 + 0.5 * inverse_square)
        far_dyadic = (inverse * inverse_square) * (0.75 - 1.5 * inverse_square)
        near_isotropic = 1.0 - (9.0 / 32.0) * (square * inverse)
        near_dyadic = (3.0 / 32.0) * inverse
        isotropic = jnp.where(far, far_isotropic, near_isotropic)
        dyadic = jnp.where(far, far_dyadic, near_dyadic)
        scaled = [dyadic * separation[a] for a in range(3)]
        for number, (a, b) in enumerate(pairs):
            entry = scaled[a] * separation[b]
            if a == b:
                entry = entry + isotropic
            for part, value in enumerate(three_parts(entry)):
                kernel_ref[number, pl.ds(part * depth + start, slab), :] = value


def mobility_body(chunks, depth, width, probe_count, home_ref, probes_ref, *refs):
    (velocity_ref, projection_ref, sources_ref,
     tile_even, tile_odd, stacked_ref, total_ref) = refs[chunks:]
    tall = 3 * probe_count
    for chunk in range(chunks):
        sources_ref[chunk] = refs[chunk][...]
    total_ref[...] = jnp.zeros_like(total_ref)
    tile_odd[...] = jnp.zeros_like(tile_odd)
    stacked_ref[...] = jnp.zeros_like(stacked_ref)

    def add_products(tile_ref, column):
        columns = pl.ds(column * width, width)
        for number, (a, b) in enumerate(pairs):
            vectors = stacked_ref[pl.ds(b * tall, tall), :]
            if a != b:
                vectors = jnp.concatenate([vectors, stacked_ref[pl.ds(a * tall, tall), :]], axis=0)
            repeated = jnp.concatenate([vectors, vectors, vectors], axis=1)
            product = lax.dot_general(
                repeated, tile_ref[number], (((1,), (0,)), ((), ())),
                preferred_element_type=jnp.float32,
            )
            total_ref[number, pl.ds(0, vectors.shape[0]), columns] += product

    def target_rows(column):
        return [home_ref[a:a + 1, column * width:(column + 1) * width] for a in range(3)]

    def chunk_step(chunk, carry):
        block = sources_ref[chunk]
        turned = jnp.transpose(block[3 * probe_count:3 * probe_count + 8])
        source_columns = [turned[:, a:a + 1] for a in range(3)]
        add_products(tile_odd, 1)
        fill_tile(tile_even, target_rows(0), source_columns, depth, 32)
        for a in range(3):
            parts = three_parts(block[a * probe_count:(a + 1) * probe_count])
            stacked_ref[pl.ds(a * tall, tall), :] = jnp.concatenate(parts, axis=0)
        add_products(tile_even, 0)
        fill_tile(tile_odd, target_rows(1), source_columns, depth, 32)
        return carry

    lax.fori_loop(0, chunks, chunk_step, 0)
    add_products(tile_odd, 1)

    def folded(number, start):
        rows = [total_ref[number, pl.ds(start + part * probe_count, probe_count), :] for part in range(3)]
        return rows[0] + (rows[1] + rows[2])

    results = [
        folded(0, 0) + folded(3, 0) + folded(4, 0),
        folded(1, 0) + folded(3, tall) + folded(5, 0),
        folded(2, 0) + folded(4, tall) + folded(5, tall),
    ]
    projection = jnp.zeros((probe_count, probe_count), jnp.float32)
    for a in range(3):
        velocity_ref[pl.ds(a * probe_count, probe_count), :] = results[a]
        projection = projection + dot_nt(results[a], probes_ref[pl.ds(a * probe_count, probe_count), :])
    projection_ref[...] = projection


def residual_body(normalizer, probe_count, mine_ref, other_ref, projection_ref, probes_ref,
                  previous_ref, beta_ref, residual_ref, gram_ref):
    projection = projection_ref[...] * normalizer
    beta = beta_ref[...]
    gram = jnp.zeros((probe_count, probe_count), jnp.float32)
    for a in range(3):
        rows = pl.ds(a * probe_count, probe_count)
        velocity = mine_ref[rows, :] + other_ref[rows, :]
        residual = velocity - dot_nn(projection, probes_ref[rows, :])
        residual = residual - dot_nn(beta, previous_ref[rows, :])
        residual_ref[rows, :] = residual
        gram = gram + dot_nt(residual, residual)
    gram_ref[...] = gram


def finish_body(normalizer, probe_count, gathered_ref, residual_ref, next_ref):
    lanes = 128
    total = jnp.sum(gathered_ref[...].reshape(-1, 8, lanes), axis=0)
    row_of = lax.broadcasted_iota(jnp.int32, (8, lanes), 0)
    even = jnp.sum(jnp.where(row_of % 2 == 0, total, 0.0), axis=0, keepdims=True)
    odd = jnp.sum(jnp.where(row_of % 2 == 1, total, 0.0), axis=0, keepdims=True)
    spread_row = lax.broadcasted_iota(jnp.int32, (probe_count, lanes), 0)
    spread_lane = lax.broadcasted_iota(jnp.int32, (probe_count, lanes), 1)
    spread = jnp.where(spread_row < 8, even, odd)
    spread = jnp.where(spread_lane // probe_count == spread_row % 8, spread, 0.0)
    picker_row = lax.broadcasted_iota(jnp.int32, (lanes, lanes), 0)
    picker_lane = lax.broadcasted_iota(jnp.int32, (lanes, lanes), 1)
    picker = jnp.where(picker_row % probe_count == picker_lane, 1.0, 0.0)
    gram = dot_nn(spread, picker) * normalizer
    work = jnp.where(spread_lane == spread_row + probe_count, 1.0, gram)
    for step in range(probe_count):
        pivot_row = work[step:step + 1, :]
        factor = work[:, step:step + 1] / work[step:step + 1, step:step + 1]
        work = work - jnp.where(spread_row > step, factor, 0.0) * pivot_row
    diagonal = jnp.sum(jnp.where(spread_lane == spread_row, work, 0.0), axis=1, keepdims=True)
    inverse_factor = (work / jnp.sqrt(diagonal))[:, probe_count:2 * probe_count]
    for a in range(3):
        rows = pl.ds(a * probe_count, probe_count)
        next_ref[rows, :] = dot_nn(inverse_factor, residual_ref[rows, :])


def on_device(body_ids, body_centers, blob_offsets, plan, probes, previous_probes, previous_beta):
    block_count = lax.axis_size("blk")
    replicas = lax.axis_size("rep")
    replica = lax.axis_index("rep")
    local_count = blob_offsets.shape[1]
    bodies = body_centers.shape[1]
    probe_count = probes.shape[1]
    tall = 3 * probe_count
    rounds = plan.shape[0]
    share = local_count // replicas
    normalizer = 1.0 / (3.0 * local_count * block_count)
    params = pltpu.CompilerParams(vmem_limit_bytes=vmem_bytes)

    member = (body_ids[None, :] == jnp.arange(bodies, dtype=jnp.int32)[:, None]).astype(jnp.float32)
    positions = jnp.dot(body_centers, member, precision=precise) + blob_offsets
    flat_probes = probes.reshape(tall, local_count)
    home = jnp.concatenate([flat_probes, positions, jnp.zeros((5, local_count), jnp.float32)], axis=0)
    payload = lax.dynamic_slice_in_dim(home, replica * share, share, 1)

    near_masks = [(x << 7) | yc for x in range(2) for yc in range(8)]
    far_masks = [z << 3 for z in range(16)]

    def exchange_by(mask):
        if mask == 0:
            return lambda value: value
        moves = [(block, block ^ mask) for block in range(block_count)]
        return lambda value: lax.ppermute(value, "blk", moves)

    near_exchanges = [exchange_by(mask) for mask in near_masks]
    far_exchanges = [exchange_by(mask) for mask in far_masks]
    near_choice = ((plan >> 7) << 3) | (plan & 7)
    far_choice = (plan >> 3) & 15

    sources = [payload]
    for number in range(rounds):
        fetched = lax.switch(near_choice[number], near_exchanges, payload)
        sources.append(lax.switch(far_choice[number], far_exchanges, fetched))

    width = local_count // 2
    velocity, projection = pl.pallas_call(
        functools.partial(mobility_body, rounds + 1, share, width, probe_count),
        out_shape=(
            jax.ShapeDtypeStruct((tall, local_count), jnp.float32),
            jax.ShapeDtypeStruct((probe_count, probe_count), jnp.float32),
        ),
        scratch_shapes=[
            pltpu.VMEM((rounds + 1,) + payload.shape, jnp.float32),
            pltpu.VMEM((6, 3 * share, width), jnp.bfloat16),
            pltpu.VMEM((6, 3 * share, width), jnp.bfloat16),
            pltpu.VMEM((3 * tall, share), jnp.bfloat16),
            pltpu.VMEM((6, 2 * tall, local_count), jnp.float32),
        ],
        compiler_params=params,
        name="mobility",
    )(positions, flat_probes, *sources)

    other_velocity = lax.ppermute(velocity, "rep", [(0, 1), (1, 0)])
    projection = projection + lax.ppermute(projection, "rep", [(0, 1), (1, 0)])
    bit = 1
    while bit < block_count:
        projection = projection + exchange_by(bit)(projection)
        bit = 2 * bit

    residual, gram = pl.pallas_call(
        functools.partial(residual_body, normalizer, probe_count),
        out_shape=(
            jax.ShapeDtypeStruct((tall, local_count), jnp.float32),
            jax.ShapeDtypeStruct((probe_count, probe_count), jnp.float32),
        ),
        compiler_params=params,
        name="residual",
    )(velocity, other_velocity, projection, flat_probes, previous_probes.reshape(tall, local_count), previous_beta)

    near_groups = [[mask ^ z for mask in near_masks] for z in far_masks]
    far_groups = [[z ^ mask for z in far_masks] for mask in near_masks]

    def spread_to(value, groups):
        copies = jnp.broadcast_to(value[None], (len(groups[0]),) + value.shape)
        return lax.all_to_all(copies, "blk", 0, 0, axis_index_groups=groups)

    gram = gram.reshape(2, probe_count * probe_count // 2)
    gram = jnp.sum(spread_to(gram, near_groups), axis=0)
    gathered = spread_to(gram, far_groups)
    result = pl.pallas_call(
        functools.partial(finish_body, normalizer, probe_count),
        out_shape=jax.ShapeDtypeStruct((tall, local_count), jnp.float32),
        compiler_params=params,
        name="finish",
    )(gathered.reshape(-1, gathered.shape[-1]), residual)
    return result.reshape(probes.shape)


def solution(mesh):
    in_specs = (P("blk"), P(), P(None, "blk"), P(), P(None, None, "blk"), P(None, None, "blk"), P())
    out_specs = P(None, None, "blk")
    return jax.shard_map(
        on_device, mesh=mesh, in_specs=in_specs, out_specs=out_specs, check_vma=False
    )
```

```python
import functools

import jax
import jax.numpy as jnp
from jax import lax
from jax.experimental import pallas as pl
from jax.experimental.pallas import tpu as pltpu
from jax.sharding import PartitionSpec as P

precise = lax.Precision.HIGHEST
pairs = ((0, 0), (1, 1), (2, 2), (0, 1), (0, 2), (1, 2))
vmem_bytes = 40 * 1024 * 1024


def two_parts(value):
    high = value.astype(jnp.bfloat16)
    return high, (value - high.astype(jnp.float32)).astype(jnp.bfloat16)


def dot_nt(left, right):
    return lax.dot_general(
        left, right, (((1,), (1,)), ((), ())), precision=precise,
        preferred_element_type=jnp.float32,
    )


def dot_nn(left, right):
    return lax.dot_general(
        left, right, (((1,), (0,)), ((), ())), precision=precise,
        preferred_element_type=jnp.float32,
    )


def fill_tile(kernel_ref, target_rows, source_columns, depth, slab):
    for start in range(0, depth, slab):
        rows = slice(start, start + slab)
        separation = [target_rows[a] - source_columns[a][rows] for a in range(3)]
        square = separation[0] * separation[0]
        square = square + separation[1] * separation[1]
        square = square + separation[2] * separation[2]
        inverse = lax.rsqrt(jnp.where(square > 0.0, square, 1.0))
        inverse_square = inverse * inverse
        far = square > 4.0
        far_isotropic = inverse * (0.75 + 0.5 * inverse_square)
        far_dyadic = (inverse * inverse_square) * (0.75 - 1.5 * inverse_square)
        near_isotropic = 1.0 - (9.0 / 32.0) * (square * inverse)
        near_dyadic = (3.0 / 32.0) * inverse
        isotropic = jnp.where(far, far_isotropic, near_isotropic)
        dyadic = jnp.where(far, far_dyadic, near_dyadic)
        scaled = [dyadic * separation[a] for a in range(3)]
        for number, (a, b) in enumerate(pairs):
            entry = scaled[a] * separation[b]
            if a == b:
                entry = entry + isotropic
            for part, value in enumerate(two_parts(entry)):
                kernel_ref[number, pl.ds(part * depth + start, slab), :] = value


def mobility_body(chunks, depth, width, probe_count, home_ref, *refs):
    (velocity_ref, sources_ref,
     tile_even, tile_odd, stacked_ref, total_ref) = refs[chunks:]
    tall = 2 * probe_count
    for chunk in range(chunks):
        sources_ref[chunk] = refs[chunk][...]
    total_ref[...] = jnp.zeros_like(total_ref)
    tile_odd[...] = jnp.zeros_like(tile_odd)
    stacked_ref[...] = jnp.zeros_like(stacked_ref)

    def add_products(tile_ref, column):
        columns = pl.ds(column * width, width)
        for number, (a, b) in enumerate(pairs):
            vectors = stacked_ref[pl.ds(b * tall, tall), :]
            if a != b:
                vectors = jnp.concatenate([vectors, stacked_ref[pl.ds(a * tall, tall), :]], axis=0)
            repeated = jnp.concatenate([vectors, vectors], axis=1)
            product = lax.dot_general(
                repeated, tile_ref[number], (((1,), (0,)), ((), ())),
                preferred_element_type=jnp.float32,
            )
            total_ref[number, pl.ds(0, vectors.shape[0]), columns] += product

    def target_rows(column):
        return [home_ref[a:a + 1, column * width:(column + 1) * width] for a in range(3)]

    def chunk_step(chunk, carry):
        block = sources_ref[chunk]
        turned = jnp.transpose(block[3 * probe_count:3 * probe_count + 8])
        source_columns = [turned[:, a:a + 1] for a in range(3)]
        add_products(tile_odd, 1)
        fill_tile(tile_even, target_rows(0), source_columns, depth, 32)
        for a in range(3):
            parts = two_parts(block[a * probe_count:(a + 1) * probe_count])
            stacked_ref[pl.ds(a * tall, tall), :] = jnp.concatenate(parts, axis=0)
        add_products(tile_even, 0)
        fill_tile(tile_odd, target_rows(1), source_columns, depth, 32)
        return carry

    lax.fori_loop(0, chunks, chunk_step, 0)
    add_products(tile_odd, 1)

    def folded(number, start):
        rows = [total_ref[number, pl.ds(start + part * probe_count, probe_count), :] for part in range(2)]
        return rows[0] + rows[1]

    results = [
        folded(0, 0) + folded(3, 0) + folded(4, 0),
        folded(1, 0) + folded(3, tall) + folded(5, 0),
        folded(2, 0) + folded(4, tall) + folded(5, tall),
    ]
    for a in range(3):
        velocity_ref[pl.ds(a * probe_count, probe_count), :] = results[a]


def moments_body(probe_count, mine_ref, other_ref, probes_ref, previous_ref, beta_ref,
                 velocity_ref, moments_ref):
    beta = beta_ref[...]
    total = jnp.zeros((probe_count, 4 * probe_count), jnp.float32)
    lane = lax.broadcasted_iota(jnp.int32, total.shape, 1)
    for a in range(3):
        rows = pl.ds(a * probe_count, probe_count)
        probes = probes_ref[rows, :]
        velocity = mine_ref[rows, :] + other_ref[rows, :]
        reduced = velocity - dot_nn(beta, previous_ref[rows, :])
        velocity_ref[rows, :] = reduced
        stack = jnp.concatenate([velocity, reduced, probes, reduced], axis=0)
        both = dot_nt(jnp.concatenate([probes, reduced], axis=0), stack)
        total = total + jnp.where(lane < 3 * probe_count, both[:probe_count], both[probe_count:])
    half = probe_count // 2
    moments_ref[...] = jnp.concatenate([total[:half], total[half:]], axis=1)


def apply_factor(gram, residuals, next_ref, identity):
    probe_count = gram.shape[0]
    work = jnp.concatenate([gram, identity], axis=1)
    row_of = lax.broadcasted_iota(jnp.int32, work.shape, 0)
    lane_of = lax.broadcasted_iota(jnp.int32, work.shape, 1)
    for step in range(probe_count):
        pivot_row = work[step:step + 1, :]
        factor = work[:, step:step + 1] / work[step:step + 1, step:step + 1]
        work = work - jnp.where(row_of > step, factor, 0.0) * pivot_row
    pivots = jnp.sum(jnp.where(lane_of == row_of, work, 0.0), axis=1, keepdims=True)
    inverse_factor = (work / jnp.sqrt(pivots))[:, probe_count:2 * probe_count]
    for a in range(3):
        next_ref[pl.ds(a * probe_count, probe_count), :] = dot_nn(inverse_factor, residuals[a])
    return pivots


def unit_matrix(size):
    rows = lax.broadcasted_iota(jnp.int32, (size, size), 0)
    return jnp.where(rows == lax.broadcasted_iota(jnp.int32, (size, size), 1), 1.0, 0.0)


def finish_body(normalizer, probe_count, slots, limit, gathered_ref, probes_ref, velocity_ref,
                next_ref, residual_ref, flag_ref):
    packed = jnp.sum(gathered_ref[...].reshape(slots, probe_count // 2, 8 * probe_count), axis=0)
    packed = packed * normalizer
    moments = jnp.concatenate([packed[:, :4 * probe_count], packed[:, 4 * probe_count:]], axis=0)
    projection, cross, probe_gram, velocity_gram = [
        moments[:, k * probe_count:(k + 1) * probe_count] for k in range(4)
    ]
    identity = unit_matrix(probe_count)
    turned = dot_nt(identity, projection)
    mixed = dot_nn(turned, cross)
    square = dot_nn(turned, dot_nn(probe_gram, projection))
    gram = velocity_gram - mixed - dot_nt(identity, mixed) + square
    residuals = []
    for a in range(3):
        rows = pl.ds(a * probe_count, probe_count)
        residuals.append(velocity_ref[rows, :] - dot_nn(turned, probes_ref[rows, :]))
        residual_ref[rows, :] = residuals[a]
    pivots = apply_factor(gram, residuals, next_ref, identity)
    terms = jnp.sum((velocity_gram + square) * identity, axis=1, keepdims=True)
    unsafe = jnp.max(jnp.where(terms <= limit * pivots, 0.0, 1.0))
    flag_ref[0] = (unsafe > 0.0).astype(jnp.int32)


def gram_body(probe_count, residual_ref, gram_ref):
    gram = jnp.zeros((probe_count, probe_count), jnp.float32)
    for a in range(3):
        residual = residual_ref[pl.ds(a * probe_count, probe_count), :]
        gram = gram + dot_nt(residual, residual)
    half = probe_count // 2
    gram_ref[...] = jnp.concatenate([gram[:half], gram[half:]], axis=1)


def refactor_body(normalizer, probe_count, slots, gathered_ref, residual_ref, next_ref):
    packed = jnp.sum(gathered_ref[...].reshape(slots, probe_count // 2, 2 * probe_count), axis=0)
    packed = packed * normalizer
    gram = jnp.concatenate([packed[:, :probe_count], packed[:, probe_count:]], axis=0)
    residuals = [residual_ref[pl.ds(a * probe_count, probe_count), :] for a in range(3)]
    apply_factor(gram, residuals, next_ref, unit_matrix(probe_count))


def on_device(body_ids, body_centers, blob_offsets, plan, probes, previous_probes, previous_beta):
    block_count = lax.axis_size("blk")
    replicas = lax.axis_size("rep")
    replica = lax.axis_index("rep")
    local_count = blob_offsets.shape[1]
    bodies = body_centers.shape[1]
    probe_count = probes.shape[1]
    tall = 3 * probe_count
    rounds = plan.shape[0]
    share = local_count // replicas
    normalizer = 1.0 / (3.0 * local_count * block_count)
    params = pltpu.CompilerParams(vmem_limit_bytes=vmem_bytes)

    member = (body_ids[None, :] == jnp.arange(bodies, dtype=jnp.int32)[:, None]).astype(jnp.float32)
    positions = jnp.dot(body_centers, member, precision=precise) + blob_offsets
    flat_probes = probes.reshape(tall, local_count)
    home = jnp.concatenate([flat_probes, positions, jnp.zeros((5, local_count), jnp.float32)], axis=0)
    payload = lax.dynamic_slice_in_dim(home, replica * share, share, 1)

    bit_count = block_count.bit_length() - 1
    near_masks = [(x << (bit_count - 1)) | yc for x in range(2) for yc in range(8)]
    far_masks = [z << 3 for z in range(block_count // 16)]

    def exchange_by(mask):
        if mask == 0:
            return lambda value: value
        moves = [(block, block ^ mask) for block in range(block_count)]
        return lambda value: lax.ppermute(value, "blk", moves)

    near_exchanges = [exchange_by(mask) for mask in near_masks]
    far_exchanges = [exchange_by(mask) for mask in far_masks]
    shifts = 8 * jnp.arange(rounds, dtype=jnp.int32)
    packed_plan = jnp.sum(plan.astype(jnp.int32) << shifts)

    sources = [payload]
    for number in range(rounds):
        pattern = packed_plan >> (8 * number)
        near_choice = ((pattern >> (bit_count - 4)) & 8) | (pattern & 7)
        far_choice = (pattern >> 3) & (len(far_masks) - 1)
        fetched = lax.switch(near_choice, near_exchanges, payload)
        sources.append(lax.switch(far_choice, far_exchanges, fetched))

    width = local_count // 2
    flat = jax.ShapeDtypeStruct((tall, local_count), jnp.float32)

    def kernel_call(body, out_shape, name, **options):
        return pl.pallas_call(body, out_shape=out_shape, compiler_params=params, name=name, **options)

    velocity = kernel_call(
        functools.partial(mobility_body, rounds + 1, share, width, probe_count), flat, "mobility",
        scratch_shapes=[
            pltpu.VMEM((rounds + 1,) + payload.shape, jnp.float32),
            pltpu.VMEM((6, 2 * share, width), jnp.bfloat16),
            pltpu.VMEM((6, 2 * share, width), jnp.bfloat16),
            pltpu.VMEM((6 * probe_count, share), jnp.bfloat16),
            pltpu.VMEM((6, 4 * probe_count, local_count), jnp.float32),
        ],
    )(positions, *sources)
    other_velocity = lax.ppermute(velocity, "rep", [(0, 1), (1, 0)])

    near_groups = [[mask ^ z for mask in near_masks] for z in far_masks]
    far_groups = [[z ^ mask for z in far_masks] for mask in near_masks]
    slots = len(far_masks)

    def spread_to(value, groups):
        copies = jnp.broadcast_to(value[None], (len(groups[0]),) + value.shape)
        return lax.all_to_all(copies, "blk", 0, 0, axis_index_groups=groups)

    def gathered_sums(value):
        return spread_to(jnp.sum(spread_to(value, near_groups), axis=0), far_groups)

    reduced, moments = kernel_call(
        functools.partial(moments_body, probe_count),
        (flat, jax.ShapeDtypeStruct((probe_count // 2, 8 * probe_count), jnp.float32)), "moments",
    )(velocity, other_velocity, flat_probes, previous_probes.reshape(tall, local_count), previous_beta)
    result, residual, flag = kernel_call(
        functools.partial(finish_body, normalizer, probe_count, slots, 64.0),
        (flat, flat, jax.ShapeDtypeStruct((1,), jnp.int32)), "finish",
        out_specs=(
            pl.BlockSpec(memory_space=pltpu.VMEM),
            pl.BlockSpec(memory_space=pltpu.VMEM),
            pl.BlockSpec(memory_space=pltpu.SMEM),
        ),
    )(gathered_sums(moments), flat_probes, reduced)

    def from_residual(result, residual):
        gram = kernel_call(
            functools.partial(gram_body, probe_count),
            jax.ShapeDtypeStruct((probe_count // 2, 2 * probe_count), jnp.float32), "gram",
        )(residual)
        return kernel_call(
            functools.partial(refactor_body, normalizer, probe_count, slots), flat, "refactor",
        )(gathered_sums(gram), residual)

    result = lax.cond(flag[0] > 0, from_residual, lambda result, residual: result, result, residual)
    return result.reshape(probes.shape)


def solution(mesh):
    in_specs = (P("blk"), P(), P(None, "blk"), P(), P(None, None, "blk"), P(None, None, "blk"), P())
    out_specs = P(None, None, "blk")
    return jax.shard_map(
        on_device, mesh=mesh, in_specs=in_specs, out_specs=out_specs, check_vma=False
    )
```

```python
import functools

import jax
import jax.numpy as jnp
from jax import lax
from jax.experimental import pallas as pl
from jax.experimental.pallas import tpu as pltpu
from jax.sharding import PartitionSpec as P

precise = lax.Precision.HIGHEST
pairs = ((0, 0), (1, 1), (2, 2), (0, 1), (0, 2), (1, 2))
vmem_bytes = 40 * 1024 * 1024


def two_parts(value):
    high = value.astype(jnp.bfloat16)
    return high, (value - high.astype(jnp.float32)).astype(jnp.bfloat16)


def dot_nt(left, right):
    return lax.dot_general(
        left, right, (((1,), (1,)), ((), ())), precision=precise,
        preferred_element_type=jnp.float32,
    )


def dot_nn(left, right):
    return lax.dot_general(
        left, right, (((1,), (0,)), ((), ())), precision=precise,
        preferred_element_type=jnp.float32,
    )


def fill_tile(kernel_ref, target_rows, source_columns, depth, slab):
    for start in range(0, depth, slab):
        rows = slice(start, start + slab)
        separation = [target_rows[a] - source_columns[a][rows] for a in range(3)]
        square = separation[0] * separation[0]
        square = square + separation[1] * separation[1]
        square = square + separation[2] * separation[2]
        inverse = lax.rsqrt(jnp.where(square > 0.0, square, 1.0))
        inverse_square = inverse * inverse
        far = square > 4.0
        far_isotropic = inverse * (0.75 + 0.5 * inverse_square)
        far_dyadic = (inverse * inverse_square) * (0.75 - 1.5 * inverse_square)
        near_isotropic = 1.0 - (9.0 / 32.0) * (square * inverse)
        near_dyadic = (3.0 / 32.0) * inverse
        isotropic = jnp.where(far, far_isotropic, near_isotropic)
        dyadic = jnp.where(far, far_dyadic, near_dyadic)
        scaled = [dyadic * separation[a] for a in range(3)]
        for number, (a, b) in enumerate(pairs):
            entry = scaled[a] * separation[b]
            if a == b:
                entry = entry + isotropic
            for part, value in enumerate(two_parts(entry)):
                kernel_ref[number, pl.ds(part * depth + start, slab), :] = value


def mobility_body(chunks, replicas, depth, width, probe_count, home_ref, *refs):
    (velocity_ref, sources_ref,
     tile_even, tile_odd, stacked_ref, total_ref) = refs[-6:]
    tall = 2 * probe_count
    sources_ref[0] = refs[0][...]
    for chunk in range(1, chunks):
        block_ref = refs[1 + (chunk - 1) // replicas]
        start = (chunk - 1) % replicas * depth
        sources_ref[chunk] = block_ref[:, start:start + depth]
    total_ref[...] = jnp.zeros_like(total_ref)
    tile_odd[...] = jnp.zeros_like(tile_odd)
    stacked_ref[...] = jnp.zeros_like(stacked_ref)

    def add_products(tile_ref, column):
        columns = pl.ds(column * width, width)
        for number, (a, b) in enumerate(pairs):
            vectors = stacked_ref[pl.ds(b * tall, tall), :]
            if a != b:
                vectors = jnp.concatenate([vectors, stacked_ref[pl.ds(a * tall, tall), :]], axis=0)
            repeated = jnp.concatenate([vectors, vectors], axis=1)
            product = lax.dot_general(
                repeated, tile_ref[number], (((1,), (0,)), ((), ())),
                preferred_element_type=jnp.float32,
            )
            total_ref[number, pl.ds(0, vectors.shape[0]), columns] += product

    def target_rows(column):
        return [home_ref[a:a + 1, column * width:(column + 1) * width] for a in range(3)]

    def chunk_step(chunk, carry):
        block = sources_ref[chunk]
        turned = jnp.transpose(block[3 * probe_count:3 * probe_count + 8])
        source_columns = [turned[:, a:a + 1] for a in range(3)]
        add_products(tile_odd, 1)
        fill_tile(tile_even, target_rows(0), source_columns, depth, 32)
        for a in range(3):
            parts = two_parts(block[a * probe_count:(a + 1) * probe_count])
            stacked_ref[pl.ds(a * tall, tall), :] = jnp.concatenate(parts, axis=0)
        add_products(tile_even, 0)
        fill_tile(tile_odd, target_rows(1), source_columns, depth, 32)
        return carry

    lax.fori_loop(0, chunks, chunk_step, 0)
    add_products(tile_odd, 1)

    def folded(number, start):
        rows = [total_ref[number, pl.ds(start + part * probe_count, probe_count), :] for part in range(2)]
        return rows[0] + rows[1]

    results = [
        folded(0, 0) + folded(3, 0) + folded(4, 0),
        folded(1, 0) + folded(3, tall) + folded(5, 0),
        folded(2, 0) + folded(4, tall) + folded(5, tall),
    ]
    for a in range(3):
        velocity_ref[pl.ds(a * probe_count, probe_count), :] = results[a]


def moments_body(probe_count, mine_ref, other_ref, probes_ref, previous_ref, beta_ref,
                 velocity_ref, moments_ref):
    beta = beta_ref[...]
    total = jnp.zeros((probe_count, 4 * probe_count), jnp.float32)
    lane = lax.broadcasted_iota(jnp.int32, total.shape, 1)
    for a in range(3):
        rows = pl.ds(a * probe_count, probe_count)
        probes = probes_ref[rows, :]
        velocity = mine_ref[rows, :] + other_ref[rows, :]
        reduced = velocity - dot_nn(beta, previous_ref[rows, :])
        velocity_ref[rows, :] = reduced
        stack = jnp.concatenate([velocity, reduced, probes, reduced], axis=0)
        both = dot_nt(jnp.concatenate([probes, reduced], axis=0), stack)
        total = total + jnp.where(lane < 3 * probe_count, both[:probe_count], both[probe_count:])
    half = probe_count // 2
    moments_ref[...] = jnp.concatenate([total[:half], total[half:]], axis=1)


def apply_factor(gram, residuals, next_ref, identity):
    probe_count = gram.shape[0]
    work = jnp.concatenate([gram, identity], axis=1)
    row_of = lax.broadcasted_iota(jnp.int32, work.shape, 0)
    lane_of = lax.broadcasted_iota(jnp.int32, work.shape, 1)
    for step in range(probe_count):
        pivot_row = work[step:step + 1, :]
        factor = work[:, step:step + 1] / work[step:step + 1, step:step + 1]
        work = work - jnp.where(row_of > step, factor, 0.0) * pivot_row
    pivots = jnp.sum(jnp.where(lane_of == row_of, work, 0.0), axis=1, keepdims=True)
    inverse_factor = (work / jnp.sqrt(pivots))[:, probe_count:2 * probe_count]
    for a in range(3):
        next_ref[pl.ds(a * probe_count, probe_count), :] = dot_nn(inverse_factor, residuals[a])
    return pivots


def unit_matrix(size):
    rows = lax.broadcasted_iota(jnp.int32, (size, size), 0)
    return jnp.where(rows == lax.broadcasted_iota(jnp.int32, (size, size), 1), 1.0, 0.0)


def finish_body(normalizer, probe_count, slots, limit, gathered_ref, probes_ref, velocity_ref,
                next_ref, residual_ref, flag_ref):
    packed = jnp.sum(gathered_ref[...].reshape(slots, probe_count // 2, 8 * probe_count), axis=0)
    packed = packed * normalizer
    moments = jnp.concatenate([packed[:, :4 * probe_count], packed[:, 4 * probe_count:]], axis=0)
    projection, cross, probe_gram, velocity_gram = [
        moments[:, k * probe_count:(k + 1) * probe_count] for k in range(4)
    ]
    identity = unit_matrix(probe_count)
    turned = dot_nt(identity, projection)
    mixed = dot_nn(turned, cross)
    square = dot_nn(turned, dot_nn(probe_gram, projection))
    gram = velocity_gram - mixed - dot_nt(identity, mixed) + square
    residuals = []
    for a in range(3):
        rows = pl.ds(a * probe_count, probe_count)
        residuals.append(velocity_ref[rows, :] - dot_nn(turned, probes_ref[rows, :]))
        residual_ref[rows, :] = residuals[a]
    pivots = apply_factor(gram, residuals, next_ref, identity)
    terms = jnp.sum((velocity_gram + square) * identity, axis=1, keepdims=True)
    unsafe = jnp.max(jnp.where(terms <= limit * pivots, 0.0, 1.0))
    flag_ref[0] = (unsafe > 0.0).astype(jnp.int32)


def gram_body(probe_count, residual_ref, gram_ref):
    gram = jnp.zeros((probe_count, probe_count), jnp.float32)
    for a in range(3):
        residual = residual_ref[pl.ds(a * probe_count, probe_count), :]
        gram = gram + dot_nt(residual, residual)
    half = probe_count // 2
    gram_ref[...] = jnp.concatenate([gram[:half], gram[half:]], axis=1)


def refactor_body(normalizer, probe_count, slots, gathered_ref, residual_ref, next_ref):
    packed = jnp.sum(gathered_ref[...].reshape(slots, probe_count // 2, 2 * probe_count), axis=0)
    packed = packed * normalizer
    gram = jnp.concatenate([packed[:, :probe_count], packed[:, probe_count:]], axis=0)
    residuals = [residual_ref[pl.ds(a * probe_count, probe_count), :] for a in range(3)]
    apply_factor(gram, residuals, next_ref, unit_matrix(probe_count))


def on_device(body_ids, body_centers, blob_offsets, plan, probes, previous_probes, previous_beta):
    block_count = lax.axis_size("blk")
    replicas = lax.axis_size("rep")
    replica = lax.axis_index("rep")
    local_count = blob_offsets.shape[1]
    bodies = body_centers.shape[1]
    probe_count = probes.shape[1]
    tall = 3 * probe_count
    rounds = plan.shape[0]
    share = local_count // replicas
    normalizer = 1.0 / (3.0 * local_count * block_count)
    params = pltpu.CompilerParams(vmem_limit_bytes=vmem_bytes)

    member = (body_ids[None, :] == jnp.arange(bodies, dtype=jnp.int32)[:, None]).astype(jnp.float32)
    positions = jnp.dot(body_centers, member, precision=precise) + blob_offsets
    flat_probes = probes.reshape(tall, local_count)
    home = jnp.concatenate([flat_probes, positions, jnp.zeros((5, local_count), jnp.float32)], axis=0)
    own_share = lax.dynamic_slice_in_dim(home, replica * share, share, 1)
    per_replica = rounds // replicas
    chunks = 1 + per_replica * replicas

    bit_count = block_count.bit_length() - 1
    near_masks = [(x << (bit_count - 1)) | yc for x in range(2) for yc in range(8)]
    far_masks = [z << 3 for z in range(block_count // 16)]

    def exchange_by(mask):
        if mask == 0:
            return lambda value: value
        moves = [(block, block ^ mask) for block in range(block_count)]
        return lambda value: lax.ppermute(value, "blk", moves)

    near_exchanges = [exchange_by(mask) for mask in near_masks]
    far_exchanges = [exchange_by(mask) for mask in far_masks]
    place = jnp.arange(rounds, dtype=jnp.int32) - replica * per_replica
    mine = (place >= 0) & (place < per_replica)
    packed_plan = jnp.sum(jnp.where(mine, plan << (8 * jnp.where(mine, place, 0)), 0))

    sources = [own_share]
    for number in range(per_replica):
        pattern = packed_plan >> (8 * number)
        near_choice = ((pattern >> (bit_count - 4)) & 8) | (pattern & 7)
        far_choice = (pattern >> 3) & (len(far_masks) - 1)
        fetched = lax.switch(near_choice, near_exchanges, home)
        sources.append(lax.switch(far_choice, far_exchanges, fetched))

    width = local_count // 2
    flat = jax.ShapeDtypeStruct((tall, local_count), jnp.float32)

    def kernel_call(body, out_shape, name, **options):
        return pl.pallas_call(body, out_shape=out_shape, compiler_params=params, name=name, **options)

    velocity = kernel_call(
        functools.partial(mobility_body, chunks, replicas, share, width, probe_count), flat, "mobility",
        scratch_shapes=[
            pltpu.VMEM((chunks,) + own_share.shape, jnp.float32),
            pltpu.VMEM((6, 2 * share, width), jnp.bfloat16),
            pltpu.VMEM((6, 2 * share, width), jnp.bfloat16),
            pltpu.VMEM((6 * probe_count, share), jnp.bfloat16),
            pltpu.VMEM((6, 4 * probe_count, local_count), jnp.float32),
        ],
    )(positions, *sources)
    other_velocity = lax.ppermute(velocity, "rep", [(0, 1), (1, 0)])

    near_groups = [[mask ^ z for mask in near_masks] for z in far_masks]
    far_groups = [[z ^ mask for z in far_masks] for mask in near_masks]
    slots = len(far_masks)

    def spread_to(value, groups):
        copies = jnp.broadcast_to(value[None], (len(groups[0]),) + value.shape)
        return lax.all_to_all(copies, "blk", 0, 0, axis_index_groups=groups)

    def gathered_sums(value):
        return spread_to(jnp.sum(spread_to(value, near_groups), axis=0), far_groups)

    reduced, moments = kernel_call(
        functools.partial(moments_body, probe_count),
        (flat, jax.ShapeDtypeStruct((probe_count // 2, 8 * probe_count), jnp.float32)), "moments",
    )(velocity, other_velocity, flat_probes, previous_probes.reshape(tall, local_count), previous_beta)
    result, residual, flag = kernel_call(
        functools.partial(finish_body, normalizer, probe_count, slots, 64.0),
        (flat, flat, jax.ShapeDtypeStruct((1,), jnp.int32)), "finish",
        out_specs=(
            pl.BlockSpec(memory_space=pltpu.VMEM),
            pl.BlockSpec(memory_space=pltpu.VMEM),
            pl.BlockSpec(memory_space=pltpu.SMEM),
        ),
    )(gathered_sums(moments), flat_probes, reduced)

    def from_residual(result, residual):
        gram = kernel_call(
            functools.partial(gram_body, probe_count),
            jax.ShapeDtypeStruct((probe_count // 2, 2 * probe_count), jnp.float32), "gram",
        )(residual)
        return kernel_call(
            functools.partial(refactor_body, normalizer, probe_count, slots), flat, "refactor",
        )(gathered_sums(gram), residual)

    result = lax.cond(flag[0] > 0, from_residual, lambda result, residual: result, result, residual)
    return result.reshape(probes.shape)


def solution(mesh):
    in_specs = (P("blk"), P(), P(None, "blk"), P(), P(None, None, "blk"), P(None, None, "blk"), P())
    out_specs = P(None, None, "blk")
    return jax.shard_map(
        on_device, mesh=mesh, in_specs=in_specs, out_specs=out_specs, check_vma=False
    )
```

```python
import functools

import jax
import jax.numpy as jnp
from jax import lax
from jax.experimental import pallas as pl
from jax.experimental.pallas import tpu as pltpu
from jax.sharding import PartitionSpec as P

precise = lax.Precision.HIGHEST
pairs = ((0, 0), (1, 1), (2, 2), (0, 1), (0, 2), (1, 2))
vmem_bytes = 40 * 1024 * 1024


def two_parts(value):
    high = value.astype(jnp.bfloat16)
    return high, (value - high.astype(jnp.float32)).astype(jnp.bfloat16)


def dot_nt(left, right):
    return lax.dot_general(
        left, right, (((1,), (1,)), ((), ())), precision=precise,
        preferred_element_type=jnp.float32,
    )


def dot_nn(left, right):
    return lax.dot_general(
        left, right, (((1,), (0,)), ((), ())), precision=precise,
        preferred_element_type=jnp.float32,
    )


def fill_tile(kernel_ref, target_rows, source_columns, depth, slab):
    for start in range(0, depth, slab):
        rows = slice(start, start + slab)
        separation = [target_rows[a] - source_columns[a][rows] for a in range(3)]
        square = separation[0] * separation[0]
        square = square + separation[1] * separation[1]
        square = square + separation[2] * separation[2]
        inverse = lax.rsqrt(jnp.where(square > 0.0, square, 1.0))
        inverse_square = inverse * inverse
        far = square > 4.0
        far_isotropic = inverse * (0.75 + 0.5 * inverse_square)
        far_dyadic = (inverse * inverse_square) * (0.75 - 1.5 * inverse_square)
        near_isotropic = 1.0 - (9.0 / 32.0) * (square * inverse)
        near_dyadic = (3.0 / 32.0) * inverse
        isotropic = jnp.where(far, far_isotropic, near_isotropic)
        dyadic = jnp.where(far, far_dyadic, near_dyadic)
        scaled = [dyadic * separation[a] for a in range(3)]
        for number, (a, b) in enumerate(pairs):
            entry = scaled[a] * separation[b]
            if a == b:
                entry = entry + isotropic
            for part, value in enumerate(two_parts(entry)):
                kernel_ref[number, pl.ds(part * depth + start, slab), :] = value


def mobility_body(layout, with_partial, depth, width, probe_count, home_ref, *refs):
    (velocity_ref, sources_ref, tile_even, tile_odd, stacked_ref, total_ref) = refs[-6:]
    chunks = len(layout)
    tall = 2 * probe_count
    for chunk, (number, start) in enumerate(layout):
        sources_ref[chunk] = refs[number][:, start:start + depth]
    total_ref[...] = jnp.zeros_like(total_ref)
    tile_odd[...] = jnp.zeros_like(tile_odd)
    stacked_ref[...] = jnp.zeros_like(stacked_ref)

    def add_products(tile_ref, column):
        columns = pl.ds(column * width, width)
        for number, (a, b) in enumerate(pairs):
            vectors = stacked_ref[pl.ds(b * tall, tall), :]
            if a != b:
                vectors = jnp.concatenate([vectors, stacked_ref[pl.ds(a * tall, tall), :]], axis=0)
            repeated = jnp.concatenate([vectors, vectors], axis=1)
            product = lax.dot_general(
                repeated, tile_ref[number], (((1,), (0,)), ((), ())),
                preferred_element_type=jnp.float32,
            )
            total_ref[number, pl.ds(0, vectors.shape[0]), columns] += product

    def target_rows(column):
        return [home_ref[a:a + 1, column * width:(column + 1) * width] for a in range(3)]

    def chunk_step(chunk, carry):
        block = sources_ref[chunk]
        turned = jnp.transpose(block[3 * probe_count:3 * probe_count + 8])
        source_columns = [turned[:, a:a + 1] for a in range(3)]
        add_products(tile_odd, 1)
        fill_tile(tile_even, target_rows(0), source_columns, depth, 32)
        for a in range(3):
            parts = two_parts(block[a * probe_count:(a + 1) * probe_count])
            stacked_ref[pl.ds(a * tall, tall), :] = jnp.concatenate(parts, axis=0)
        add_products(tile_even, 0)
        fill_tile(tile_odd, target_rows(1), source_columns, depth, 32)
        return carry

    lax.fori_loop(0, chunks, chunk_step, 0)
    add_products(tile_odd, 1)

    def folded(number, start):
        rows = [total_ref[number, pl.ds(start + part * probe_count, probe_count), :] for part in range(2)]
        return rows[0] + rows[1]

    results = [
        folded(0, 0) + folded(3, 0) + folded(4, 0),
        folded(1, 0) + folded(3, tall) + folded(5, 0),
        folded(2, 0) + folded(4, tall) + folded(5, tall),
    ]
    for a in range(3):
        rows = pl.ds(a * probe_count, probe_count)
        if with_partial:
            velocity_ref[rows, :] = refs[-7][rows, :] + results[a]
        else:
            velocity_ref[rows, :] = results[a]


def moments_body(probe_count, mine_ref, other_ref, probes_ref, previous_ref, beta_ref,
                 velocity_ref, moments_ref):
    beta = beta_ref[...]
    total = jnp.zeros((probe_count, 4 * probe_count), jnp.float32)
    lane = lax.broadcasted_iota(jnp.int32, total.shape, 1)
    for a in range(3):
        rows = pl.ds(a * probe_count, probe_count)
        probes = probes_ref[rows, :]
        velocity = mine_ref[rows, :] + other_ref[rows, :]
        reduced = velocity - dot_nn(beta, previous_ref[rows, :])
        velocity_ref[rows, :] = reduced
        stack = jnp.concatenate([velocity, reduced, probes, reduced], axis=0)
        both = dot_nt(jnp.concatenate([probes, reduced], axis=0), stack)
        total = total + jnp.where(lane < 3 * probe_count, both[:probe_count], both[probe_count:])
    half = probe_count // 2
    moments_ref[...] = jnp.concatenate([total[:half], total[half:]], axis=1)


def apply_factor(gram, residuals, next_ref, identity):
    probe_count = gram.shape[0]
    work = jnp.concatenate([gram, identity], axis=1)
    row_of = lax.broadcasted_iota(jnp.int32, work.shape, 0)
    lane_of = lax.broadcasted_iota(jnp.int32, work.shape, 1)
    for step in range(probe_count):
        pivot_row = work[step:step + 1, :]
        factor = work[:, step:step + 1] / work[step:step + 1, step:step + 1]
        work = work - jnp.where(row_of > step, factor, 0.0) * pivot_row
    pivots = jnp.sum(jnp.where(lane_of == row_of, work, 0.0), axis=1, keepdims=True)
    inverse_factor = (work / jnp.sqrt(pivots))[:, probe_count:2 * probe_count]
    for a in range(3):
        next_ref[pl.ds(a * probe_count, probe_count), :] = dot_nn(inverse_factor, residuals[a])
    return pivots


def unit_matrix(size):
    rows = lax.broadcasted_iota(jnp.int32, (size, size), 0)
    return jnp.where(rows == lax.broadcasted_iota(jnp.int32, (size, size), 1), 1.0, 0.0)


def finish_body(normalizer, probe_count, slots, limit, gathered_ref, probes_ref, velocity_ref,
                next_ref, residual_ref, flag_ref):
    packed = jnp.sum(gathered_ref[...].reshape(slots, probe_count // 2, 8 * probe_count), axis=0)
    packed = packed * normalizer
    moments = jnp.concatenate([packed[:, :4 * probe_count], packed[:, 4 * probe_count:]], axis=0)
    projection, cross, probe_gram, velocity_gram = [
        moments[:, k * probe_count:(k + 1) * probe_count] for k in range(4)
    ]
    identity = unit_matrix(probe_count)
    turned = dot_nt(identity, projection)
    mixed = dot_nn(turned, cross)
    square = dot_nn(turned, dot_nn(probe_gram, projection))
    gram = velocity_gram - mixed - dot_nt(identity, mixed) + square
    residuals = []
    for a in range(3):
        rows = pl.ds(a * probe_count, probe_count)
        residuals.append(velocity_ref[rows, :] - dot_nn(turned, probes_ref[rows, :]))
        residual_ref[rows, :] = residuals[a]
    pivots = apply_factor(gram, residuals, next_ref, identity)
    terms = jnp.sum((velocity_gram + square) * identity, axis=1, keepdims=True)
    unsafe = jnp.max(jnp.where(terms <= limit * pivots, 0.0, 1.0))
    flag_ref[0] = (unsafe > 0.0).astype(jnp.int32)


def gram_body(probe_count, residual_ref, gram_ref):
    gram = jnp.zeros((probe_count, probe_count), jnp.float32)
    for a in range(3):
        residual = residual_ref[pl.ds(a * probe_count, probe_count), :]
        gram = gram + dot_nt(residual, residual)
    half = probe_count // 2
    gram_ref[...] = jnp.concatenate([gram[:half], gram[half:]], axis=1)


def refactor_body(normalizer, probe_count, slots, gathered_ref, residual_ref, next_ref):
    packed = jnp.sum(gathered_ref[...].reshape(slots, probe_count // 2, 2 * probe_count), axis=0)
    packed = packed * normalizer
    gram = jnp.concatenate([packed[:, :probe_count], packed[:, probe_count:]], axis=0)
    residuals = [residual_ref[pl.ds(a * probe_count, probe_count), :] for a in range(3)]
    apply_factor(gram, residuals, next_ref, unit_matrix(probe_count))


def on_device(body_ids, body_centers, blob_offsets, plan, probes, previous_probes, previous_beta):
    block_count = lax.axis_size("blk")
    replicas = lax.axis_size("rep")
    replica = lax.axis_index("rep")
    local_count = blob_offsets.shape[1]
    bodies = body_centers.shape[1]
    probe_count = probes.shape[1]
    tall = 3 * probe_count
    rounds = plan.shape[0]
    share = local_count // replicas
    normalizer = 1.0 / (3.0 * local_count * block_count)
    params = pltpu.CompilerParams(vmem_limit_bytes=vmem_bytes)

    member = (body_ids[None, :] == jnp.arange(bodies, dtype=jnp.int32)[:, None]).astype(jnp.float32)
    positions = jnp.dot(body_centers, member, precision=precise) + blob_offsets
    flat_probes = probes.reshape(tall, local_count)
    home = jnp.concatenate([flat_probes, positions, jnp.zeros((5, local_count), jnp.float32)], axis=0)
    own_share = lax.dynamic_slice_in_dim(home, replica * share, share, 1)

    bit_count = block_count.bit_length() - 1
    near_masks = [(x << (bit_count - 1)) | yc for x in range(2) for yc in range(8)]
    far_masks = [z << 3 for z in range(block_count // 16)]

    def exchange_by(mask):
        if mask == 0:
            return lambda value: value
        moves = [(block, block ^ mask) for block in range(block_count)]
        return lambda value: lax.ppermute(value, "blk", moves)

    near_exchanges = [exchange_by(mask) for mask in near_masks]
    far_exchanges = [exchange_by(mask) for mask in far_masks]
    far_limit = len(far_masks) - 1
    near_all = ((plan >> (bit_count - 4)) & 8) | (plan & 7)
    far_all = (plan >> 3) & far_limit
    weight = jnp.where(far_all > 0, 2, 0) + jnp.where(near_all > 0, 1, 0)
    weight = weight * rounds + jnp.arange(rounds, dtype=jnp.int32)
    rank = jnp.sum((weight[None, :] > weight[:, None]).astype(jnp.int32), axis=1)
    turn, seat = rank // replicas, rank % replicas
    seat = jnp.where(turn % 2 == 0, seat, replicas - 1 - seat)
    packed_plan = jnp.sum(jnp.where(seat == replica, plan << (8 * turn), 0))

    def choices(number):
        pattern = packed_plan >> (8 * number)
        near = ((pattern >> (bit_count - 4)) & 8) | (pattern & 7)
        return near, (pattern >> 3) & far_limit

    width = local_count // 2
    flat = jax.ShapeDtypeStruct((tall, local_count), jnp.float32)

    def kernel_call(body, out_shape, name, **options):
        return pl.pallas_call(body, out_shape=out_shape, compiler_params=params, name=name, **options)

    def mobility(layout, operands, partial=None):
        chunks = len(layout)
        pair_count = chunks * share * local_count
        return kernel_call(
            functools.partial(mobility_body, layout, partial is not None, share, width, probe_count),
            flat, "mobility",
            scratch_shapes=[
                pltpu.VMEM((chunks,) + own_share.shape, jnp.float32),
                pltpu.VMEM((6, 2 * share, width), jnp.bfloat16),
                pltpu.VMEM((6, 2 * share, width), jnp.bfloat16),
                pltpu.VMEM((6 * probe_count, share), jnp.bfloat16),
                pltpu.VMEM((6, 4 * probe_count, local_count), jnp.float32),
            ],
            cost_estimate=pl.CostEstimate(
                flops=pair_count * 2000, bytes_accessed=pair_count // 2, transcendentals=pair_count
            ),
        )(positions, *operands, *([] if partial is None else [partial]))

    whole = tuple(range(0, local_count, share))
    first_layout = ((0, 0),) + tuple((1, start) for start in whole)
    later_layout = tuple((0, start) for start in whole)

    def two_exchanges(far, near):
        return lambda fetched, home: (far_exchanges[far](fetched), near_exchanges[near](home))

    def exchange_beside_products(far):
        def branch(fetched, block, own_share):
            arriving = far_exchanges[far](fetched)
            return arriving, mobility(first_layout, (own_share, block))
        return branch

    near_first, far_first = choices(0)
    near_second, far_second = choices(1)
    fetched = lax.switch(near_first, near_exchanges, home)
    block, fetched = lax.switch(
        far_first * len(near_masks) + near_second,
        [two_exchanges(far, near) for far in range(len(far_masks)) for near in range(len(near_masks))],
        fetched, home,
    )
    arriving, velocity = lax.switch(
        far_second, [exchange_beside_products(far) for far in range(len(far_masks))],
        fetched, block, own_share,
    )
    velocity = mobility(later_layout, (arriving,), velocity)
    other_velocity = lax.ppermute(velocity, "rep", [(0, 1), (1, 0)])

    near_groups = [[mask ^ z for mask in near_masks] for z in far_masks]
    far_groups = [[z ^ mask for z in far_masks] for mask in near_masks]
    slots = len(far_masks)

    def spread_to(value, groups):
        copies = jnp.broadcast_to(value[None], (len(groups[0]),) + value.shape)
        return lax.all_to_all(copies, "blk", 0, 0, axis_index_groups=groups)

    def gathered_sums(value):
        return spread_to(jnp.sum(spread_to(value, near_groups), axis=0), far_groups)

    reduced, moments = kernel_call(
        functools.partial(moments_body, probe_count),
        (flat, jax.ShapeDtypeStruct((probe_count // 2, 8 * probe_count), jnp.float32)), "moments",
    )(velocity, other_velocity, flat_probes, previous_probes.reshape(tall, local_count), previous_beta)
    result, residual, flag = kernel_call(
        functools.partial(finish_body, normalizer, probe_count, slots, 64.0),
        (flat, flat, jax.ShapeDtypeStruct((1,), jnp.int32)), "finish",
        out_specs=(
            pl.BlockSpec(memory_space=pltpu.VMEM),
            pl.BlockSpec(memory_space=pltpu.VMEM),
            pl.BlockSpec(memory_space=pltpu.SMEM),
        ),
    )(gathered_sums(moments), flat_probes, reduced)

    def from_residual(result, residual):
        gram = kernel_call(
            functools.partial(gram_body, probe_count),
            jax.ShapeDtypeStruct((probe_count // 2, 2 * probe_count), jnp.float32), "gram",
        )(residual)
        return kernel_call(
            functools.partial(refactor_body, normalizer, probe_count, slots), flat, "refactor",
        )(gathered_sums(gram), residual)

    result = lax.cond(flag[0] > 0, from_residual, lambda result, residual: result, result, residual)
    return result.reshape(probes.shape)


def solution(mesh):
    in_specs = (P("blk"), P(), P(None, "blk"), P(), P(None, None, "blk"), P(None, None, "blk"), P())
    out_specs = P(None, None, "blk")
    return jax.shard_map(
        on_device, mesh=mesh, in_specs=in_specs, out_specs=out_specs, check_vma=False
    )
```

```python
import functools

import jax
import jax.numpy as jnp
from jax import lax
from jax.experimental import pallas as pl
from jax.experimental.pallas import tpu as pltpu
from jax.sharding import PartitionSpec as P

precise = lax.Precision.HIGHEST
pairs = ((0, 0), (1, 1), (2, 2), (0, 1), (0, 2), (1, 2))
vmem_bytes = 40 * 1024 * 1024


def two_parts(value):
    high = value.astype(jnp.bfloat16)
    return high, (value - high.astype(jnp.float32)).astype(jnp.bfloat16)


def dot_nt(left, right):
    return lax.dot_general(
        left, right, (((1,), (1,)), ((), ())), precision=precise,
        preferred_element_type=jnp.float32,
    )


def dot_nn(left, right):
    return lax.dot_general(
        left, right, (((1,), (0,)), ((), ())), precision=precise,
        preferred_element_type=jnp.float32,
    )


def fill_tile(kernel_ref, target_rows, source_columns, depth, slab, between):
    for start in range(0, depth, slab):
        if between:
            between.pop(0)()
        rows = slice(start, start + slab)
        separation = [target_rows[a] - source_columns[a][rows] for a in range(3)]
        square = separation[0] * separation[0]
        square = square + separation[1] * separation[1]
        square = square + separation[2] * separation[2]
        inverse = lax.rsqrt(jnp.where(square > 0.0, square, 1.0))
        inverse_square = inverse * inverse
        far = square > 4.0
        far_isotropic = inverse * (0.75 + 0.5 * inverse_square)
        far_dyadic = (inverse * inverse_square) * (0.75 - 1.5 * inverse_square)
        near_isotropic = 1.0 - (9.0 / 32.0) * (square * inverse)
        near_dyadic = (3.0 / 32.0) * inverse
        isotropic = jnp.where(far, far_isotropic, near_isotropic)
        dyadic = jnp.where(far, far_dyadic, near_dyadic)
        scaled = [dyadic * separation[a] for a in range(3)]
        for number, (a, b) in enumerate(pairs):
            entry = scaled[a] * separation[b]
            if a == b:
                entry = entry + isotropic
            for part, value in enumerate(two_parts(entry)):
                kernel_ref[number, pl.ds(part * depth + start, slab), :] = value
    for call in between:
        call()


def mobility_body(chunks, replicas, depth, width, probe_count, home_ref, *refs):
    (velocity_ref, sources_ref,
     tile_even, tile_odd, stacked_ref, total_ref) = refs[-6:]
    tall = 2 * probe_count
    sources_ref[0] = refs[0][...]
    for chunk in range(1, chunks):
        block_ref = refs[1 + (chunk - 1) // replicas]
        start = (chunk - 1) % replicas * depth
        sources_ref[chunk] = block_ref[:, start:start + depth]
    total_ref[...] = jnp.zeros_like(total_ref)
    tile_odd[...] = jnp.zeros_like(tile_odd)
    stacked_ref[...] = jnp.zeros_like(stacked_ref)

    def add_product(tile_ref, column, number):
        a, b = pairs[number]
        vectors = stacked_ref[pl.ds(b * tall, tall), :]
        if a != b:
            vectors = jnp.concatenate([vectors, stacked_ref[pl.ds(a * tall, tall), :]], axis=0)
        repeated = jnp.concatenate([vectors, vectors], axis=1)
        product = lax.dot_general(
            repeated, tile_ref[number], (((1,), (0,)), ((), ())),
            preferred_element_type=jnp.float32,
        )
        total_ref[number, pl.ds(0, vectors.shape[0]), pl.ds(column * width, width)] += product

    def products(tile_ref, column):
        return [functools.partial(add_product, tile_ref, column, number) for number in range(len(pairs))]

    def target_rows(column):
        return [home_ref[a:a + 1, column * width:(column + 1) * width] for a in range(3)]

    def chunk_step(chunk, carry):
        block = sources_ref[chunk]
        turned = jnp.transpose(block[3 * probe_count:3 * probe_count + 8])
        source_columns = [turned[:, a:a + 1] for a in range(3)]
        fill_tile(tile_even, target_rows(0), source_columns, depth, 32, products(tile_odd, 1))
        for a in range(3):
            parts = two_parts(block[a * probe_count:(a + 1) * probe_count])
            stacked_ref[pl.ds(a * tall, tall), :] = jnp.concatenate(parts, axis=0)
        fill_tile(tile_odd, target_rows(1), source_columns, depth, 32, products(tile_even, 0))
        return carry

    lax.fori_loop(0, chunks, chunk_step, 0)
    for call in products(tile_odd, 1):
        call()

    def folded(number, start):
        rows = [total_ref[number, pl.ds(start + part * probe_count, probe_count), :] for part in range(2)]
        return rows[0] + rows[1]

    results = [
        folded(0, 0) + folded(3, 0) + folded(4, 0),
        folded(1, 0) + folded(3, tall) + folded(5, 0),
        folded(2, 0) + folded(4, tall) + folded(5, tall),
    ]
    for a in range(3):
        velocity_ref[pl.ds(a * probe_count, probe_count), :] = results[a]


def moments_body(probe_count, mine_ref, other_ref, probes_ref, previous_ref, beta_ref,
                 velocity_ref, moments_ref):
    beta = beta_ref[...]
    total = jnp.zeros((probe_count, 4 * probe_count), jnp.float32)
    lane = lax.broadcasted_iota(jnp.int32, total.shape, 1)
    for a in range(3):
        rows = pl.ds(a * probe_count, probe_count)
        probes = probes_ref[rows, :]
        velocity = mine_ref[rows, :] + other_ref[rows, :]
        reduced = velocity - dot_nn(beta, previous_ref[rows, :])
        velocity_ref[rows, :] = reduced
        stack = jnp.concatenate([velocity, reduced, probes, reduced], axis=0)
        both = dot_nt(jnp.concatenate([probes, reduced], axis=0), stack)
        total = total + jnp.where(lane < 3 * probe_count, both[:probe_count], both[probe_count:])
    half = probe_count // 2
    moments_ref[...] = jnp.concatenate([total[:half], total[half:]], axis=1)


def apply_factor(gram, residuals, next_ref, identity):
    probe_count = gram.shape[0]
    work = jnp.concatenate([gram, identity], axis=1)
    row_of = lax.broadcasted_iota(jnp.int32, work.shape, 0)
    lane_of = lax.broadcasted_iota(jnp.int32, work.shape, 1)
    for step in range(probe_count):
        pivot_row = work[step:step + 1, :]
        factor = work[:, step:step + 1] / work[step:step + 1, step:step + 1]
        work = work - jnp.where(row_of > step, factor, 0.0) * pivot_row
    pivots = jnp.sum(jnp.where(lane_of == row_of, work, 0.0), axis=1, keepdims=True)
    inverse_factor = (work / jnp.sqrt(pivots))[:, probe_count:2 * probe_count]
    for a in range(3):
        next_ref[pl.ds(a * probe_count, probe_count), :] = dot_nn(inverse_factor, residuals[a])
    return pivots


def unit_matrix(size):
    rows = lax.broadcasted_iota(jnp.int32, (size, size), 0)
    return jnp.where(rows == lax.broadcasted_iota(jnp.int32, (size, size), 1), 1.0, 0.0)


def finish_body(normalizer, probe_count, slots, limit, gathered_ref, probes_ref, velocity_ref,
                next_ref, residual_ref, flag_ref):
    packed = jnp.sum(gathered_ref[...].reshape(slots, probe_count // 2, 8 * probe_count), axis=0)
    packed = packed * normalizer
    moments = jnp.concatenate([packed[:, :4 * probe_count], packed[:, 4 * probe_count:]], axis=0)
    projection, cross, probe_gram, velocity_gram = [
        moments[:, k * probe_count:(k + 1) * probe_count] for k in range(4)
    ]
    identity = unit_matrix(probe_count)
    turned = dot_nt(identity, projection)
    mixed = dot_nn(turned, cross)
    square = dot_nn(turned, dot_nn(probe_gram, projection))
    gram = velocity_gram - mixed - dot_nt(identity, mixed) + square
    residuals = []
    for a in range(3):
        rows = pl.ds(a * probe_count, probe_count)
        residuals.append(velocity_ref[rows, :] - dot_nn(turned, probes_ref[rows, :]))
        residual_ref[rows, :] = residuals[a]
    pivots = apply_factor(gram, residuals, next_ref, identity)
    terms = jnp.sum((velocity_gram + square) * identity, axis=1, keepdims=True)
    unsafe = jnp.max(jnp.where(terms <= limit * pivots, 0.0, 1.0))
    flag_ref[0] = (unsafe > 0.0).astype(jnp.int32)


def gram_body(probe_count, residual_ref, gram_ref):
    gram = jnp.zeros((probe_count, probe_count), jnp.float32)
    for a in range(3):
        residual = residual_ref[pl.ds(a * probe_count, probe_count), :]
        gram = gram + dot_nt(residual, residual)
    half = probe_count // 2
    gram_ref[...] = jnp.concatenate([gram[:half], gram[half:]], axis=1)


def refactor_body(normalizer, probe_count, slots, gathered_ref, residual_ref, next_ref):
    packed = jnp.sum(gathered_ref[...].reshape(slots, probe_count // 2, 2 * probe_count), axis=0)
    packed = packed * normalizer
    gram = jnp.concatenate([packed[:, :probe_count], packed[:, probe_count:]], axis=0)
    residuals = [residual_ref[pl.ds(a * probe_count, probe_count), :] for a in range(3)]
    apply_factor(gram, residuals, next_ref, unit_matrix(probe_count))


def on_device(body_ids, body_centers, blob_offsets, plan, probes, previous_probes, previous_beta):
    block_count = lax.axis_size("blk")
    replicas = lax.axis_size("rep")
    replica = lax.axis_index("rep")
    local_count = blob_offsets.shape[1]
    bodies = body_centers.shape[1]
    probe_count = probes.shape[1]
    tall = 3 * probe_count
    rounds = plan.shape[0]
    share = local_count // replicas
    normalizer = 1.0 / (3.0 * local_count * block_count)
    params = pltpu.CompilerParams(vmem_limit_bytes=vmem_bytes)

    member = (body_ids[None, :] == jnp.arange(bodies, dtype=jnp.int32)[:, None]).astype(jnp.float32)
    positions = jnp.dot(body_centers, member, precision=precise) + blob_offsets
    flat_probes = probes.reshape(tall, local_count)
    home = jnp.concatenate([flat_probes, positions, jnp.zeros((5, local_count), jnp.float32)], axis=0)
    own_share = lax.dynamic_slice_in_dim(home, replica * share, share, 1)
    per_replica = rounds // replicas
    chunks = 1 + per_replica * replicas

    bit_count = block_count.bit_length() - 1
    near_masks = [(x << (bit_count - 1)) | yc for x in range(2) for yc in range(8)]
    far_masks = [z << 3 for z in range(block_count // 16)]

    def exchange_by(mask):
        if mask == 0:
            return lambda value: value
        moves = [(block, block ^ mask) for block in range(block_count)]
        return lambda value: lax.ppermute(value, "blk", moves)

    near_exchanges = [exchange_by(mask) for mask in near_masks]
    far_exchanges = [exchange_by(mask) for mask in far_masks]
    far_limit = len(far_masks) - 1
    near_all = ((plan >> (bit_count - 4)) & 8) | (plan & 7)
    weight = jnp.where((plan >> 3) & far_limit > 0, 2, 0) + jnp.where(near_all > 0, 1, 0)
    weight = weight * rounds + jnp.arange(rounds, dtype=jnp.int32)
    rank = jnp.sum((weight[None, :] > weight[:, None]).astype(jnp.int32), axis=1)
    turn, seat = rank // replicas, rank % replicas
    seat = jnp.where(turn % 2 == 0, seat, replicas - 1 - seat)
    packed_plan = jnp.sum(jnp.where(seat == replica, plan << (8 * turn), 0))

    sources = [own_share]
    for number in range(per_replica):
        pattern = packed_plan >> (8 * number)
        near_choice = ((pattern >> (bit_count - 4)) & 8) | (pattern & 7)
        far_choice = (pattern >> 3) & far_limit
        fetched = lax.switch(near_choice, near_exchanges, home)
        sources.append(lax.switch(far_choice, far_exchanges, fetched))

    width = local_count // 2
    flat = jax.ShapeDtypeStruct((tall, local_count), jnp.float32)

    def kernel_call(body, out_shape, name, **options):
        return pl.pallas_call(body, out_shape=out_shape, compiler_params=params, name=name, **options)

    velocity = kernel_call(
        functools.partial(mobility_body, chunks, replicas, share, width, probe_count), flat, "mobility",
        scratch_shapes=[
            pltpu.VMEM((chunks,) + own_share.shape, jnp.float32),
            pltpu.VMEM((6, 2 * share, width), jnp.bfloat16),
            pltpu.VMEM((6, 2 * share, width), jnp.bfloat16),
            pltpu.VMEM((6 * probe_count, share), jnp.bfloat16),
            pltpu.VMEM((6, 4 * probe_count, local_count), jnp.float32),
        ],
    )(positions, *sources)
    other_velocity = lax.ppermute(velocity, "rep", [(0, 1), (1, 0)])

    near_groups = [[mask ^ z for mask in near_masks] for z in far_masks]
    beside, apart = far_masks[:4], far_masks[::4]
    beside_groups = [[base ^ near ^ mask for mask in beside] for base in apart for near in near_masks]
    apart_groups = [[base ^ near ^ mask for mask in apart] for base in beside for near in near_masks]
    slots = len(apart)

    def spread_to(value, groups):
        copies = jnp.broadcast_to(value[None], (len(groups[0]),) + value.shape)
        return lax.all_to_all(copies, "blk", 0, 0, axis_index_groups=groups)

    def gathered_sums(value):
        for groups in (near_groups, beside_groups):
            value = jnp.sum(spread_to(value, groups), axis=0)
        return spread_to(value, apart_groups)

    reduced, moments = kernel_call(
        functools.partial(moments_body, probe_count),
        (flat, jax.ShapeDtypeStruct((probe_count // 2, 8 * probe_count), jnp.float32)), "moments",
    )(velocity, other_velocity, flat_probes, previous_probes.reshape(tall, local_count), previous_beta)
    result, residual, flag = kernel_call(
        functools.partial(finish_body, normalizer, probe_count, slots, 64.0),
        (flat, flat, jax.ShapeDtypeStruct((1,), jnp.int32)), "finish",
        out_specs=(
            pl.BlockSpec(memory_space=pltpu.VMEM),
            pl.BlockSpec(memory_space=pltpu.VMEM),
            pl.BlockSpec(memory_space=pltpu.SMEM),
        ),
    )(gathered_sums(moments), flat_probes, reduced)

    def from_residual(result, residual):
        gram = kernel_call(
            functools.partial(gram_body, probe_count),
            jax.ShapeDtypeStruct((probe_count // 2, 2 * probe_count), jnp.float32), "gram",
        )(residual)
        return kernel_call(
            functools.partial(refactor_body, normalizer, probe_count, slots), flat, "refactor",
        )(gathered_sums(gram), residual)

    result = lax.cond(flag[0] > 0, from_residual, lambda result, residual: result, result, residual)
    return result.reshape(probes.shape)


def solution(mesh):
    in_specs = (P("blk"), P(), P(None, "blk"), P(), P(None, None, "blk"), P(None, None, "blk"), P())
    out_specs = P(None, None, "blk")
    return jax.shard_map(
        on_device, mesh=mesh, in_specs=in_specs, out_specs=out_specs, check_vma=False
    )
```

```python
import functools

import jax
import jax.numpy as jnp
from jax import lax
from jax.experimental import pallas as pl
from jax.experimental.pallas import tpu as pltpu
from jax.sharding import PartitionSpec as P

precise = lax.Precision.HIGHEST
pairs = ((0, 0), (1, 1), (2, 2), (0, 1), (0, 2), (1, 2))
vmem_bytes = 40 * 1024 * 1024


def two_parts(value):
    high = value.astype(jnp.bfloat16)
    return high, (value - high.astype(jnp.float32)).astype(jnp.bfloat16)


def dot_nt(left, right):
    return lax.dot_general(
        left, right, (((1,), (1,)), ((), ())), precision=precise,
        preferred_element_type=jnp.float32,
    )


def dot_nn(left, right):
    return lax.dot_general(
        left, right, (((1,), (0,)), ((), ())), precision=precise,
        preferred_element_type=jnp.float32,
    )


def fill_tile(kernel_ref, target_rows, source_columns, depth, slab, between):
    for start in range(0, depth, slab):
        if between:
            between.pop(0)()
        rows = slice(start, start + slab)
        separation = [target_rows[a] - source_columns[a][rows] for a in range(3)]
        square = separation[0] * separation[0]
        square = square + separation[1] * separation[1]
        square = square + separation[2] * separation[2]
        inverse = lax.rsqrt(jnp.where(square > 0.0, square, 1.0))
        inverse_square = inverse * inverse
        far = square > 4.0
        far_isotropic = inverse * (0.75 + 0.5 * inverse_square)
        far_dyadic = (inverse * inverse_square) * (0.75 - 1.5 * inverse_square)
        near_isotropic = 1.0 - (9.0 / 32.0) * (square * inverse)
        near_dyadic = (3.0 / 32.0) * inverse
        isotropic = jnp.where(far, far_isotropic, near_isotropic)
        dyadic = jnp.where(far, far_dyadic, near_dyadic)
        scaled = [dyadic * separation[a] for a in range(3)]
        for number, (a, b) in enumerate(pairs):
            entry = scaled[a] * separation[b]
            if a == b:
                entry = entry + isotropic
            for part, value in enumerate(two_parts(entry)):
                kernel_ref[number, pl.ds(part * depth + start, slab), :] = value
    for call in between:
        call()


def pack_body(probe_count, ids_ref, centers_ref, offsets_ref, probes_ref, positions_ref, packed_ref):
    ids = ids_ref[...]
    bodies, count = centers_ref.shape[1], ids.shape[1]
    member = lax.broadcasted_iota(jnp.int32, (bodies, count), 0) == ids
    member = jnp.where(member, 1.0, 0.0).astype(jnp.bfloat16)
    centers = centers_ref[...]
    high, middle = two_parts(centers)
    low = ((centers - high.astype(jnp.float32)) - middle.astype(jnp.float32)).astype(jnp.bfloat16)
    chosen = [
        lax.dot_general(part, member, (((1,), (0,)), ((), ())), preferred_element_type=jnp.float32)
        for part in (high, middle, low)
    ]
    positions = ((chosen[0] + chosen[1]) + chosen[2]) + offsets_ref[...]
    positions_ref[...] = positions
    tall, lanes = 3 * probe_count, 128
    stride = 2 * tall + 8
    for group in range(count // (2 * lanes)):
        left, right = slice(2 * group * lanes, (2 * group + 1) * lanes), slice((2 * group + 1) * lanes, (2 * group + 2) * lanes)
        packed_ref[pl.ds(group * stride, tall), :] = probes_ref[:, left]
        packed_ref[pl.ds(group * stride + tall, tall), :] = probes_ref[:, right]
        packed_ref[pl.ds(group * stride + 2 * tall, 3), :] = positions[:, left]
        packed_ref[pl.ds(group * stride + 2 * tall + 3, 3), :] = positions[:, right]
        packed_ref[pl.ds(group * stride + 2 * tall + 6, 2), :] = jnp.zeros((2, lanes), jnp.float32)


def mobility_body(block_total, depth, width, probe_count, chunks_ref, home_ref, *refs):
    blocks = refs[:block_total]
    (velocity_ref, sources_ref, tile_even, tile_odd, stacked_ref, total_ref, arrived) = refs[block_total:]
    tall = 2 * probe_count
    stride = 6 * probe_count + 8
    copies = [
        pltpu.make_async_copy(blocks[number], sources_ref.at[number], arrived.at[number])
        for number in range(block_total)
    ]
    for copy in copies:
        copy.start()
    total_ref[...] = jnp.zeros_like(total_ref)
    tile_odd[...] = jnp.zeros_like(tile_odd)
    stacked_ref[...] = jnp.zeros_like(stacked_ref)
    for copy in copies:
        copy.wait()

    def add_product(tile_ref, column, number):
        a, b = pairs[number]
        vectors = stacked_ref[pl.ds(b * tall, tall), :]
        if a != b:
            vectors = jnp.concatenate([vectors, stacked_ref[pl.ds(a * tall, tall), :]], axis=0)
        repeated = jnp.concatenate([vectors, vectors], axis=1)
        product = lax.dot_general(
            repeated, tile_ref[number], (((1,), (0,)), ((), ())),
            preferred_element_type=jnp.float32,
        )
        total_ref[number, pl.ds(0, vectors.shape[0]), pl.ds(column * width, width)] += product

    def products(tile_ref, column):
        return [functools.partial(add_product, tile_ref, column, number) for number in range(len(pairs))]

    def target_rows(column):
        return [home_ref[a:a + 1, column * width:(column + 1) * width] for a in range(3)]

    def chunk_step(chunk, carry):
        block = sources_ref[chunk // 2, pl.ds(pl.multiple_of(chunk % 2 * stride, 8), stride), :]
        turned = jnp.transpose(block[6 * probe_count:])
        source_columns = [
            jnp.concatenate([turned[:, a:a + 1], turned[:, 3 + a:4 + a]], axis=0) for a in range(3)
        ]
        vectors = jnp.concatenate([block[:3 * probe_count], block[3 * probe_count:6 * probe_count]], axis=1)
        fill_tile(tile_even, target_rows(0), source_columns, depth, 32, products(tile_odd, 1))
        for a in range(3):
            parts = two_parts(vectors[a * probe_count:(a + 1) * probe_count])
            stacked_ref[pl.ds(a * tall, tall), :] = jnp.concatenate(parts, axis=0)
        fill_tile(tile_odd, target_rows(1), source_columns, depth, 32, products(tile_even, 0))
        return carry

    lax.fori_loop(0, chunks_ref[0], chunk_step, 0)
    for call in products(tile_odd, 1):
        call()

    def folded(number, start):
        rows = [total_ref[number, pl.ds(start + part * probe_count, probe_count), :] for part in range(2)]
        return rows[0] + rows[1]

    results = [
        folded(0, 0) + folded(3, 0) + folded(4, 0),
        folded(1, 0) + folded(3, tall) + folded(5, 0),
        folded(2, 0) + folded(4, tall) + folded(5, tall),
    ]
    for a in range(3):
        velocity_ref[pl.ds(a * probe_count, probe_count), :] = results[a]


def moments_body(probe_count, mine_ref, other_ref, probes_ref, previous_ref, beta_ref,
                 velocity_ref, moments_ref):
    beta = beta_ref[...]
    total = jnp.zeros((probe_count, 4 * probe_count), jnp.float32)
    lane = lax.broadcasted_iota(jnp.int32, total.shape, 1)
    for a in range(3):
        rows = pl.ds(a * probe_count, probe_count)
        probes = probes_ref[rows, :]
        velocity = mine_ref[rows, :] + other_ref[rows, :]
        reduced = velocity - dot_nn(beta, previous_ref[rows, :])
        velocity_ref[rows, :] = reduced
        stack = jnp.concatenate([velocity, reduced, probes, reduced], axis=0)
        both = dot_nt(jnp.concatenate([probes, reduced], axis=0), stack)
        total = total + jnp.where(lane < 3 * probe_count, both[:probe_count], both[probe_count:])
    half = probe_count // 2
    moments_ref[...] = jnp.concatenate([total[:half], total[half:]], axis=1)


def apply_factor(gram, residuals, next_ref, identity):
    probe_count = gram.shape[0]
    work = jnp.concatenate([gram, identity], axis=1)
    row_of = lax.broadcasted_iota(jnp.int32, work.shape, 0)
    lane_of = lax.broadcasted_iota(jnp.int32, work.shape, 1)
    for step in range(probe_count):
        pivot_row = work[step:step + 1, :]
        factor = work[:, step:step + 1] / work[step:step + 1, step:step + 1]
        work = work - jnp.where(row_of > step, factor, 0.0) * pivot_row
    pivots = jnp.sum(jnp.where(lane_of == row_of, work, 0.0), axis=1, keepdims=True)
    inverse_factor = (work / jnp.sqrt(pivots))[:, probe_count:2 * probe_count]
    for a in range(3):
        next_ref[pl.ds(a * probe_count, probe_count), :] = dot_nn(inverse_factor, residuals[a])
    return pivots


def unit_matrix(size):
    rows = lax.broadcasted_iota(jnp.int32, (size, size), 0)
    return jnp.where(rows == lax.broadcasted_iota(jnp.int32, (size, size), 1), 1.0, 0.0)


def finish_body(normalizer, probe_count, slots, limit, gathered_ref, probes_ref, velocity_ref,
                next_ref, residual_ref, flag_ref):
    packed = jnp.sum(gathered_ref[...].reshape(slots, probe_count // 2, 8 * probe_count), axis=0)
    packed = packed * normalizer
    moments = jnp.concatenate([packed[:, :4 * probe_count], packed[:, 4 * probe_count:]], axis=0)
    projection, cross, probe_gram, velocity_gram = [
        moments[:, k * probe_count:(k + 1) * probe_count] for k in range(4)
    ]
    identity = unit_matrix(probe_count)
    turned = dot_nt(identity, projection)
    mixed = dot_nn(turned, cross)
    square = dot_nn(turned, dot_nn(probe_gram, projection))
    gram = velocity_gram - mixed - dot_nt(identity, mixed) + square
    residuals = []
    for a in range(3):
        rows = pl.ds(a * probe_count, probe_count)
        residuals.append(velocity_ref[rows, :] - dot_nn(turned, probes_ref[rows, :]))
        residual_ref[rows, :] = residuals[a]
    pivots = apply_factor(gram, residuals, next_ref, identity)
    terms = jnp.sum((velocity_gram + square) * identity, axis=1, keepdims=True)
    unsafe = jnp.max(jnp.where(terms <= limit * pivots, 0.0, 1.0))
    flag_ref[0] = (unsafe > 0.0).astype(jnp.int32)


def gram_body(probe_count, residual_ref, gram_ref):
    gram = jnp.zeros((probe_count, probe_count), jnp.float32)
    for a in range(3):
        residual = residual_ref[pl.ds(a * probe_count, probe_count), :]
        gram = gram + dot_nt(residual, residual)
    half = probe_count // 2
    gram_ref[...] = jnp.concatenate([gram[:half], gram[half:]], axis=1)


def refactor_body(normalizer, probe_count, slots, gathered_ref, residual_ref, next_ref):
    packed = jnp.sum(gathered_ref[...].reshape(slots, probe_count // 2, 2 * probe_count), axis=0)
    packed = packed * normalizer
    gram = jnp.concatenate([packed[:, :probe_count], packed[:, probe_count:]], axis=0)
    residuals = [residual_ref[pl.ds(a * probe_count, probe_count), :] for a in range(3)]
    apply_factor(gram, residuals, next_ref, unit_matrix(probe_count))


def on_device(body_ids, body_centers, blob_offsets, plan, probes, previous_probes, previous_beta):
    block_count = lax.axis_size("blk")
    replicas = lax.axis_size("rep")
    replica = lax.axis_index("rep")
    local_count = blob_offsets.shape[1]
    bodies = body_centers.shape[1]
    probe_count = probes.shape[1]
    tall = 3 * probe_count
    rounds = plan.shape[0]
    normalizer = 1.0 / (3.0 * local_count * block_count)
    params = pltpu.CompilerParams(vmem_limit_bytes=vmem_bytes)

    flat_probes = probes.reshape(tall, local_count)
    flat = jax.ShapeDtypeStruct((tall, local_count), jnp.float32)

    def kernel_call(body, out_shape, name, **options):
        return pl.pallas_call(body, out_shape=out_shape, compiler_params=params, name=name, **options)

    packed_rows = local_count // 256 * (2 * tall + 8)
    positions, home = kernel_call(
        functools.partial(pack_body, probe_count),
        (
            jax.ShapeDtypeStruct((3, local_count), jnp.float32),
            jax.ShapeDtypeStruct((packed_rows, 128), jnp.float32),
        ), "pack",
    )(body_ids.reshape(1, local_count), body_centers, blob_offsets, flat_probes)
    per_replica = rounds // replicas

    bit_count = block_count.bit_length() - 1
    near_masks = [(x << (bit_count - 1)) | yc for x in range(2) for yc in range(8)]
    far_masks = [z << 3 for z in range(block_count // 16)]

    def exchange_by(mask):
        if mask == 0:
            return lambda value: value
        moves = [(block, block ^ mask) for block in range(block_count)]
        return lambda value: lax.ppermute(value, "blk", moves)

    near_exchanges = [exchange_by(mask) for mask in near_masks]
    far_exchanges = [exchange_by(mask) for mask in far_masks]
    far_limit = len(far_masks) - 1
    near_all = ((plan >> (bit_count - 4)) & 8) | (plan & 7)
    weight = jnp.where((plan >> 3) & far_limit > 0, 2, 0) + jnp.where(near_all > 0, 1, 0)
    weight = weight * rounds + jnp.arange(rounds, dtype=jnp.int32)
    rank = jnp.sum((weight[None, :] > weight[:, None]).astype(jnp.int32), axis=1)
    turn, seat = rank // replicas, rank % replicas
    seat = jnp.where(turn % 2 == 0, seat, replicas - 1 - seat)
    packed_plan = jnp.sum(jnp.where(seat == replica, plan << (8 * turn), 0))

    sources = []
    for number in range(per_replica):
        pattern = packed_plan >> (8 * number)
        near_choice = ((pattern >> (bit_count - 4)) & 8) | (pattern & 7)
        far_choice = (pattern >> 3) & far_limit
        fetched = lax.switch(near_choice, near_exchanges, home)
        sources.append(lax.switch(far_choice, far_exchanges, fetched))

    depth = 256
    width = local_count // 2
    own_chunks = local_count // depth
    chunk_count = own_chunks * (per_replica + jnp.where(replica == 0, 1, 0))
    anywhere = pl.BlockSpec(memory_space=pl.ANY)
    whole = pl.BlockSpec(memory_space=pltpu.VMEM)
    velocity = kernel_call(
        functools.partial(mobility_body, per_replica + 1, depth, width, probe_count), flat, "mobility",
        in_specs=[pl.BlockSpec(memory_space=pltpu.SMEM), whole] + [anywhere] * (per_replica + 1),
        out_specs=whole,
        scratch_shapes=[
            pltpu.VMEM((per_replica + 1,) + home.shape, jnp.float32),
            pltpu.VMEM((6, 2 * depth, width), jnp.bfloat16),
            pltpu.VMEM((6, 2 * depth, width), jnp.bfloat16),
            pltpu.VMEM((6 * probe_count, depth), jnp.bfloat16),
            pltpu.VMEM((6, 4 * probe_count, local_count), jnp.float32),
            pltpu.SemaphoreType.DMA((per_replica + 1,)),
        ],
    )(chunk_count.astype(jnp.int32).reshape(1), positions, *sources, home)
    other_velocity = lax.ppermute(velocity, "rep", [(0, 1), (1, 0)])

    near_groups = [[mask ^ z for mask in near_masks] for z in far_masks]
    far_groups = [[z ^ mask for z in far_masks] for mask in near_masks]
    slots = len(far_masks)

    def spread_to(value, groups):
        copies = jnp.broadcast_to(value[None], (len(groups[0]),) + value.shape)
        return lax.all_to_all(copies, "blk", 0, 0, axis_index_groups=groups)

    def gathered_sums(value):
        return spread_to(jnp.sum(spread_to(value, near_groups), axis=0), far_groups)

    reduced, moments = kernel_call(
        functools.partial(moments_body, probe_count),
        (flat, jax.ShapeDtypeStruct((probe_count // 2, 8 * probe_count), jnp.float32)), "moments",
    )(velocity, other_velocity, flat_probes, previous_probes.reshape(tall, local_count), previous_beta)
    result, residual, flag = kernel_call(
        functools.partial(finish_body, normalizer, probe_count, slots, 64.0),
        (flat, flat, jax.ShapeDtypeStruct((1,), jnp.int32)), "finish",
        out_specs=(
            pl.BlockSpec(memory_space=pltpu.VMEM),
            pl.BlockSpec(memory_space=pltpu.VMEM),
            pl.BlockSpec(memory_space=pltpu.SMEM),
        ),
    )(gathered_sums(moments), flat_probes, reduced)

    def from_residual(result, residual):
        gram = kernel_call(
            functools.partial(gram_body, probe_count),
            jax.ShapeDtypeStruct((probe_count // 2, 2 * probe_count), jnp.float32), "gram",
        )(residual)
        return kernel_call(
            functools.partial(refactor_body, normalizer, probe_count, slots), flat, "refactor",
        )(gathered_sums(gram), residual)

    result = lax.cond(flag[0] > 0, from_residual, lambda result, residual: result, result, residual)
    return result.reshape(probes.shape)


def solution(mesh):
    in_specs = (P("blk"), P(), P(None, "blk"), P(), P(None, None, "blk"), P(None, None, "blk"), P())
    out_specs = P(None, None, "blk")
    return jax.shard_map(
        on_device, mesh=mesh, in_specs=in_specs, out_specs=out_specs, check_vma=False
    )
```

```python
import functools

import jax
import jax.numpy as jnp
from jax import lax
from jax.experimental import pallas as pl
from jax.experimental.pallas import tpu as pltpu
from jax.sharding import PartitionSpec as P

precise = lax.Precision.HIGHEST
pairs = ((0, 0), (1, 1), (2, 2), (0, 1), (0, 2), (1, 2))
vmem_bytes = 40 * 1024 * 1024


def two_parts(value):
    high = value.astype(jnp.bfloat16)
    return high, (value - high.astype(jnp.float32)).astype(jnp.bfloat16)


def dot_nt(left, right):
    return lax.dot_general(
        left, right, (((1,), (1,)), ((), ())), precision=precise,
        preferred_element_type=jnp.float32,
    )


def dot_nn(left, right):
    return lax.dot_general(
        left, right, (((1,), (0,)), ((), ())), precision=precise,
        preferred_element_type=jnp.float32,
    )


def fill_tile(kernel_ref, target_rows, source_columns, depth, slab, between):
    for start in range(0, depth, slab):
        if between:
            between.pop(0)()
        rows = slice(start, start + slab)
        separation = [target_rows[a] - source_columns[a][rows] for a in range(3)]
        square = separation[0] * separation[0]
        square = square + separation[1] * separation[1]
        square = square + separation[2] * separation[2]
        inverse = lax.rsqrt(jnp.where(square > 0.0, square, 1.0))
        inverse_square = inverse * inverse
        far = square > 4.0
        far_isotropic = inverse * (0.75 + 0.5 * inverse_square)
        far_dyadic = (inverse * inverse_square) * (0.75 - 1.5 * inverse_square)
        near_isotropic = 1.0 - (9.0 / 32.0) * (square * inverse)
        near_dyadic = (3.0 / 32.0) * inverse
        isotropic = jnp.where(far, far_isotropic, near_isotropic)
        dyadic = jnp.where(far, far_dyadic, near_dyadic)
        scaled = [dyadic * separation[a] for a in range(3)]
        for number, (a, b) in enumerate(pairs):
            entry = scaled[a] * separation[b]
            if a == b:
                entry = entry + isotropic
            for part, value in enumerate(two_parts(entry)):
                kernel_ref[number, pl.ds(part * depth + start, slab), :] = value
    for call in between:
        call()


def pack_body(probe_count, *refs):
    positions_ref, packed_ref = refs[4:6]
    ids_ref, centers_ref, offsets_ref, probes_ref = refs[6:10]
    copies = [pltpu.make_async_copy(refs[k], refs[6 + k], refs[10].at[k]) for k in range(4)]
    for copy in copies:
        copy.start()
    for copy in copies:
        copy.wait()
    ids = ids_ref[...]
    bodies, count = centers_ref.shape[1], ids.shape[1]
    member = lax.broadcasted_iota(jnp.int32, (bodies, count), 0) == ids
    member = jnp.where(member, 1.0, 0.0).astype(jnp.bfloat16)
    centers = centers_ref[...]
    high, middle = two_parts(centers)
    low = ((centers - high.astype(jnp.float32)) - middle.astype(jnp.float32)).astype(jnp.bfloat16)
    chosen = [
        lax.dot_general(part, member, (((1,), (0,)), ((), ())), preferred_element_type=jnp.float32)
        for part in (high, middle, low)
    ]
    positions = ((chosen[0] + chosen[1]) + chosen[2]) + offsets_ref[...]
    positions_ref[...] = positions
    tall, lanes = 3 * probe_count, 128
    stride = 2 * tall + 8
    for group in range(count // (2 * lanes)):
        left, right = slice(2 * group * lanes, (2 * group + 1) * lanes), slice((2 * group + 1) * lanes, (2 * group + 2) * lanes)
        packed_ref[pl.ds(group * stride, tall), :] = probes_ref[:, left]
        packed_ref[pl.ds(group * stride + tall, tall), :] = probes_ref[:, right]
        packed_ref[pl.ds(group * stride + 2 * tall, 3), :] = positions[:, left]
        packed_ref[pl.ds(group * stride + 2 * tall + 3, 3), :] = positions[:, right]
        packed_ref[pl.ds(group * stride + 2 * tall + 6, 2), :] = jnp.zeros((2, lanes), jnp.float32)


def mobility_body(chunks, depth, width, probe_count, home_ref, *refs):
    (velocity_ref, sources_ref, tile_even, tile_odd, stacked_ref, total_ref, arrived) = refs[-7:]
    tall = 2 * probe_count
    stride = 6 * probe_count + 8
    pieces = [
        block.at[pl.ds(start, stride), :]
        for block in refs[:-7] for start in range(0, block.shape[0], stride)
    ]
    copies = [
        pltpu.make_async_copy(pieces[chunk], sources_ref.at[chunk], arrived.at[chunk])
        for chunk in range(chunks)
    ]
    for copy in copies:
        copy.start()
    total_ref[...] = jnp.zeros_like(total_ref)
    tile_odd[...] = jnp.zeros_like(tile_odd)
    stacked_ref[...] = jnp.zeros_like(stacked_ref)
    for copy in copies:
        copy.wait()

    def add_product(tile_ref, column, number):
        a, b = pairs[number]
        vectors = stacked_ref[pl.ds(b * tall, tall), :]
        if a != b:
            vectors = jnp.concatenate([vectors, stacked_ref[pl.ds(a * tall, tall), :]], axis=0)
        repeated = jnp.concatenate([vectors, vectors], axis=1)
        product = lax.dot_general(
            repeated, tile_ref[number], (((1,), (0,)), ((), ())),
            preferred_element_type=jnp.float32,
        )
        total_ref[number, pl.ds(0, vectors.shape[0]), pl.ds(column * width, width)] += product

    def products(tile_ref, column):
        return [functools.partial(add_product, tile_ref, column, number) for number in range(len(pairs))]

    def target_rows(column):
        return [home_ref[a:a + 1, column * width:(column + 1) * width] for a in range(3)]

    def chunk_step(chunk, carry):
        block = sources_ref[chunk]
        turned = jnp.transpose(block[6 * probe_count:])
        source_columns = [
            jnp.concatenate([turned[:, a:a + 1], turned[:, 3 + a:4 + a]], axis=0) for a in range(3)
        ]
        vectors = jnp.concatenate([block[:3 * probe_count], block[3 * probe_count:6 * probe_count]], axis=1)
        fill_tile(tile_even, target_rows(0), source_columns, depth, 32, products(tile_odd, 1))
        for a in range(3):
            parts = two_parts(vectors[a * probe_count:(a + 1) * probe_count])
            stacked_ref[pl.ds(a * tall, tall), :] = jnp.concatenate(parts, axis=0)
        fill_tile(tile_odd, target_rows(1), source_columns, depth, 32, products(tile_even, 0))
        return carry

    lax.fori_loop(0, chunks, chunk_step, 0)
    for call in products(tile_odd, 1):
        call()

    def folded(number, start):
        rows = [total_ref[number, pl.ds(start + part * probe_count, probe_count), :] for part in range(2)]
        return rows[0] + rows[1]

    results = [
        folded(0, 0) + folded(3, 0) + folded(4, 0),
        folded(1, 0) + folded(3, tall) + folded(5, 0),
        folded(2, 0) + folded(4, tall) + folded(5, tall),
    ]
    for a in range(3):
        velocity_ref[pl.ds(a * probe_count, probe_count), :] = results[a]


def moments_body(probe_count, mine_ref, other_ref, probes_ref, previous_ref, beta_ref,
                 velocity_ref, moments_ref):
    beta = beta_ref[...]
    total = jnp.zeros((probe_count, 4 * probe_count), jnp.float32)
    lane = lax.broadcasted_iota(jnp.int32, total.shape, 1)
    for a in range(3):
        rows = pl.ds(a * probe_count, probe_count)
        probes = probes_ref[rows, :]
        velocity = mine_ref[rows, :] + other_ref[rows, :]
        reduced = velocity - dot_nn(beta, previous_ref[rows, :])
        velocity_ref[rows, :] = reduced
        stack = jnp.concatenate([velocity, reduced, probes, reduced], axis=0)
        both = dot_nt(jnp.concatenate([probes, reduced], axis=0), stack)
        total = total + jnp.where(lane < 3 * probe_count, both[:probe_count], both[probe_count:])
    half = probe_count // 2
    moments_ref[...] = jnp.concatenate([total[:half], total[half:]], axis=1)


def apply_factor(gram, residuals, next_ref, identity):
    probe_count = gram.shape[0]
    work = jnp.concatenate([gram, identity], axis=1)
    row_of = lax.broadcasted_iota(jnp.int32, work.shape, 0)
    lane_of = lax.broadcasted_iota(jnp.int32, work.shape, 1)
    for step in range(probe_count):
        pivot_row = work[step:step + 1, :]
        factor = work[:, step:step + 1] / work[step:step + 1, step:step + 1]
        work = work - jnp.where(row_of > step, factor, 0.0) * pivot_row
    pivots = jnp.sum(jnp.where(lane_of == row_of, work, 0.0), axis=1, keepdims=True)
    inverse_factor = (work / jnp.sqrt(pivots))[:, probe_count:2 * probe_count]
    for a in range(3):
        next_ref[pl.ds(a * probe_count, probe_count), :] = dot_nn(inverse_factor, residuals[a])
    return pivots


def unit_matrix(size):
    rows = lax.broadcasted_iota(jnp.int32, (size, size), 0)
    return jnp.where(rows == lax.broadcasted_iota(jnp.int32, (size, size), 1), 1.0, 0.0)


def finish_body(normalizer, probe_count, slots, limit, gathered_ref, probes_ref, velocity_ref,
                next_ref, residual_ref, flag_ref):
    packed = jnp.sum(gathered_ref[...].reshape(slots, probe_count // 2, 8 * probe_count), axis=0)
    packed = packed * normalizer
    moments = jnp.concatenate([packed[:, :4 * probe_count], packed[:, 4 * probe_count:]], axis=0)
    projection, cross, probe_gram, velocity_gram = [
        moments[:, k * probe_count:(k + 1) * probe_count] for k in range(4)
    ]
    identity = unit_matrix(probe_count)
    turned = dot_nt(identity, projection)
    mixed = dot_nn(turned, cross)
    square = dot_nn(turned, dot_nn(probe_gram, projection))
    gram = velocity_gram - mixed - dot_nt(identity, mixed) + square
    residuals = []
    for a in range(3):
        rows = pl.ds(a * probe_count, probe_count)
        residuals.append(velocity_ref[rows, :] - dot_nn(turned, probes_ref[rows, :]))
        residual_ref[rows, :] = residuals[a]
    pivots = apply_factor(gram, residuals, next_ref, identity)
    terms = jnp.sum((velocity_gram + square) * identity, axis=1, keepdims=True)
    unsafe = jnp.max(jnp.where(terms <= limit * pivots, 0.0, 1.0))
    flag_ref[0] = (unsafe > 0.0).astype(jnp.int32)


def gram_body(probe_count, residual_ref, gram_ref):
    gram = jnp.zeros((probe_count, probe_count), jnp.float32)
    for a in range(3):
        residual = residual_ref[pl.ds(a * probe_count, probe_count), :]
        gram = gram + dot_nt(residual, residual)
    half = probe_count // 2
    gram_ref[...] = jnp.concatenate([gram[:half], gram[half:]], axis=1)


def refactor_body(normalizer, probe_count, slots, gathered_ref, residual_ref, next_ref):
    packed = jnp.sum(gathered_ref[...].reshape(slots, probe_count // 2, 2 * probe_count), axis=0)
    packed = packed * normalizer
    gram = jnp.concatenate([packed[:, :probe_count], packed[:, probe_count:]], axis=0)
    residuals = [residual_ref[pl.ds(a * probe_count, probe_count), :] for a in range(3)]
    apply_factor(gram, residuals, next_ref, unit_matrix(probe_count))


def on_device(body_ids, body_centers, blob_offsets, plan, probes, previous_probes, previous_beta):
    block_count = lax.axis_size("blk")
    replicas = lax.axis_size("rep")
    replica = lax.axis_index("rep")
    local_count = blob_offsets.shape[1]
    bodies = body_centers.shape[1]
    probe_count = probes.shape[1]
    tall = 3 * probe_count
    rounds = plan.shape[0]
    normalizer = 1.0 / (3.0 * local_count * block_count)
    params = pltpu.CompilerParams(vmem_limit_bytes=vmem_bytes)

    flat_probes = probes.reshape(tall, local_count)
    flat = jax.ShapeDtypeStruct((tall, local_count), jnp.float32)

    def kernel_call(body, out_shape, name, **options):
        return pl.pallas_call(body, out_shape=out_shape, compiler_params=params, name=name, **options)

    packed_rows = local_count // 256 * (2 * tall + 8)
    positions, home = kernel_call(
        functools.partial(pack_body, probe_count),
        (
            jax.ShapeDtypeStruct((3, local_count), jnp.float32),
            jax.ShapeDtypeStruct((packed_rows, 128), jnp.float32),
        ), "pack",
        in_specs=[pl.BlockSpec(memory_space=pl.ANY)] * 4,
        scratch_shapes=[
            pltpu.VMEM((1, local_count), jnp.int32),
            pltpu.VMEM(body_centers.shape, jnp.float32),
            pltpu.VMEM(blob_offsets.shape, jnp.float32),
            pltpu.VMEM(flat_probes.shape, jnp.float32),
            pltpu.SemaphoreType.DMA((4,)),
        ],
    )(body_ids.reshape(1, local_count), body_centers, blob_offsets, flat_probes)

    bit_count = block_count.bit_length() - 1
    near_masks = [(x << (bit_count - 1)) | yc for x in range(2) for yc in range(8)]
    far_masks = [z << 3 for z in range(block_count // 16)]

    def exchange_by(mask):
        if mask == 0:
            return lambda value: value
        moves = [(block, block ^ mask) for block in range(block_count)]
        return lambda value: lax.ppermute(value, "blk", moves)

    near_exchanges = [exchange_by(mask) for mask in near_masks]
    far_exchanges = [exchange_by(mask) for mask in far_masks]
    far_limit = len(far_masks) - 1
    near_all = ((plan >> (bit_count - 4)) & 8) | (plan & 7)
    weight = jnp.where((plan >> 3) & far_limit > 0, 2, 0) + jnp.where(near_all > 0, 1, 0)
    weight = weight * rounds + jnp.arange(rounds, dtype=jnp.int32)
    rank = jnp.sum((weight[None, :] > weight[:, None]).astype(jnp.int32), axis=1)
    mine = jnp.where(rank < replicas, rank == replica, True)
    place = jnp.where(rank < replicas, 0, rank - replicas + 1)
    packed_plan = jnp.sum(jnp.where(mine, plan << (8 * place), 0))

    half_rows = packed_rows // replicas
    own_share = lax.dynamic_slice_in_dim(home, replica * half_rows, half_rows, 0)
    sources = []
    for number in range(rounds - replicas + 1):
        pattern = packed_plan >> (8 * number)
        near_choice = ((pattern >> (bit_count - 4)) & 8) | (pattern & 7)
        far_choice = (pattern >> 3) & far_limit
        fetched = lax.switch(near_choice, near_exchanges, own_share if number else home)
        sources.append(lax.switch(far_choice, far_exchanges, fetched))

    depth = 256
    width = local_count // 2
    sources.append(own_share)
    chunks = sum(source.shape[0] for source in sources) // half_rows
    anywhere = pl.BlockSpec(memory_space=pl.ANY)
    whole = pl.BlockSpec(memory_space=pltpu.VMEM)
    velocity = kernel_call(
        functools.partial(mobility_body, chunks, depth, width, probe_count), flat, "mobility",
        in_specs=[whole] + [anywhere] * len(sources),
        out_specs=whole,
        scratch_shapes=[
            pltpu.VMEM((chunks, half_rows, 128), jnp.float32),
            pltpu.VMEM((6, 2 * depth, width), jnp.bfloat16),
            pltpu.VMEM((6, 2 * depth, width), jnp.bfloat16),
            pltpu.VMEM((6 * probe_count, depth), jnp.bfloat16),
            pltpu.VMEM((6, 4 * probe_count, local_count), jnp.float32),
            pltpu.SemaphoreType.DMA((chunks,)),
        ],
    )(positions, *sources)
    other_velocity = lax.ppermute(velocity, "rep", [(0, 1), (1, 0)])

    near_groups = [[mask ^ z for mask in near_masks] for z in far_masks]
    far_groups = [[z ^ mask for z in far_masks] for mask in near_masks]
    slots = len(far_masks)

    def spread_to(value, groups):
        copies = jnp.broadcast_to(value[None], (len(groups[0]),) + value.shape)
        return lax.all_to_all(copies, "blk", 0, 0, axis_index_groups=groups)

    def gathered_sums(value):
        return spread_to(jnp.sum(spread_to(value, near_groups), axis=0), far_groups)

    reduced, moments = kernel_call(
        functools.partial(moments_body, probe_count),
        (flat, jax.ShapeDtypeStruct((probe_count // 2, 8 * probe_count), jnp.float32)), "moments",
    )(velocity, other_velocity, flat_probes, previous_probes.reshape(tall, local_count), previous_beta)
    result, residual, flag = kernel_call(
        functools.partial(finish_body, normalizer, probe_count, slots, 64.0),
        (flat, flat, jax.ShapeDtypeStruct((1,), jnp.int32)), "finish",
        out_specs=(
            pl.BlockSpec(memory_space=pltpu.VMEM),
            pl.BlockSpec(memory_space=pltpu.VMEM),
            pl.BlockSpec(memory_space=pltpu.SMEM),
        ),
    )(gathered_sums(moments), flat_probes, reduced)

    def from_residual(result, residual):
        gram = kernel_call(
            functools.partial(gram_body, probe_count),
            jax.ShapeDtypeStruct((probe_count // 2, 2 * probe_count), jnp.float32), "gram",
        )(residual)
        return kernel_call(
            functools.partial(refactor_body, normalizer, probe_count, slots), flat, "refactor",
        )(gathered_sums(gram), residual)

    result = lax.cond(flag[0] > 0, from_residual, lambda result, residual: result, result, residual)
    return result.reshape(probes.shape)


def solution(mesh):
    in_specs = (P("blk"), P(), P(None, "blk"), P(), P(None, None, "blk"), P(None, None, "blk"), P())
    out_specs = P(None, None, "blk")
    return jax.shard_map(
        on_device, mesh=mesh, in_specs=in_specs, out_specs=out_specs, check_vma=False
    )
```
